128 devices in a mesh: vir: 4 (over x), occ: 32 (over z, y, core).
Axes of the slice: x: 4, y: 4, z: 4, core: 2. Of those that a mesh axis runs over, the one named last changes fastest.
Arguments:
- amplitudes: bfloat16 [2304, 8, 7168], P(('vir', 'occ')), may hold values from -6 to 6
- integrals: bfloat16 [32, 7168, 1792], P('occ', 'vir'), may hold values from -0.0625 to 0.0625
- nonzero_tile_count: int32 [8], replicated, may hold values from 56 to 112, as said below
- sector_owner: int32 [8], replicated, may hold values from 0 to 7, each once
Outputs:
- residual: bfloat16 [2304, 32, 1792], P('vir', 'occ')
The draws below stay inside these ranges and needn't reach their ends.
Inputs may be any that keep to these rules, and one draw needn't show every extreme that they name: `nonzero_tile_count`: some sector has all 112 tiles live in every draw. `sector_owner`: each sector appears once.
All inputs are finite; a program needn't handle non-finite values.
Results may differ from the reference program's by a relative error of at most 0.001.
Values may be sent and summed in bfloat16 or wider, within the bound.
A program may use at most 192 MiB of HBM per device.

```python
import jax
import jax.numpy as jnp

SECTORS = 8
TILE = 64
TILES = 112
P_SIZE = 2304
QS = 7168
GROUP = 4
AB = 1792
N_OCC = 32


def draw_nonzero_tile_count(key, part):
    base = jax.random.fold_in(key, 11)
    first_key, second_key = jax.random.split(base)
    tile_counts = jax.random.randint(first_key, (SECTORS,), TILES // 2, TILES + 1)
    chosen = jax.random.randint(second_key, (), 0, SECTORS)
    tile_counts = jnp.where(jnp.arange(SECTORS) == chosen, TILES, tile_counts)
    return tile_counts.astype(jnp.int32)


def steps_of(stream_key, extent, cuts, low, top_value):
    level = 1.0
    for position, parts in cuts:
        draws = jax.random.uniform(jax.random.fold_in(jax.random.fold_in(stream_key, 6), position), (parts,), jnp.float32, low / len(cuts), top_value / len(cuts))
        level = level * jnp.repeat(jnp.exp(draws), extent[position] // parts).reshape((-1,) + (1,) * (len(extent) - 1 - position))
    return level


def noise(own_key, dims, spread, reach, pieces=(), held_as=jnp.bfloat16):
    factor_of = steps_of(own_key, dims, pieces, -0.22, 0.18) if pieces else 1.0
    drawn = jax.random.normal(own_key, dims, jnp.float32) * spread * factor_of
    return jnp.minimum(jnp.maximum(drawn, -reach), reach).astype(held_as)


def setup_inputs(seed: int = 0) -> dict:
    streams_of = jax.random.split(jax.random.key(seed), 5)
    amplitudes = noise(streams_of[0], (P_SIZE, SECTORS, QS), 1.0, 6.0, ((0, 128),))
    integrals = noise(streams_of[1], (N_OCC, QS, AB), QS ** -0.5, 0.0625, ((0, 32), (1, 4)))
    nonzero_tile_count = draw_nonzero_tile_count(jax.random.fold_in(streams_of[4], 71), 0)
    sector_owner = jax.random.permutation(streams_of[3], SECTORS).astype(jnp.int32)
    return dict(amplitudes=amplitudes, integrals=integrals, nonzero_tile_count=nonzero_tile_count, sector_owner=sector_owner)


def reference(amplitudes, integrals, nonzero_tile_count, sector_owner):
    tile_numbers = jnp.arange(QS, dtype=jnp.int32) // TILE
    results = []
    for slot_index in range(N_OCC):
        sector_id = sector_owner[slot_index // GROUP]
        live_mask = (tile_numbers < nonzero_tile_count[sector_id]).astype(jnp.bfloat16)
        masked = jnp.take(amplitudes, sector_id, axis=1) * live_mask[None, :]
        ladder_product = jnp.dot(masked, integrals[slot_index], preferred_element_type=jnp.float32)
        first_col = (slot_index % GROUP) * AB
        column_mask = live_mask[first_col:first_col + AB].astype(jnp.float32)
        results.append((ladder_product * column_mask[None, :]).astype(jnp.bfloat16))
    return jnp.stack(results, axis=1)
```

```python
import functools

import jax
import jax.numpy as jnp
from jax import lax
from jax.experimental import pallas as pl
from jax.experimental.pallas import tpu as pltpu
from jax.sharding import PartitionSpec as P

TILE = 64
MESH = pl.DeviceIdType.MESH
F32, BF16, I16, I32 = jnp.float32, jnp.bfloat16, jnp.int16, jnp.int32

ROWS = 18
SECTORS = 8
PAIR = 2 * ROWS
ZBLOCK = 4 * PAIR
HALF = 896
WIDE = 1792
LANES = 128
BLOCK = ROWS * SECTORS
TOP = 32752.0

CHUNKS = ((2,), (1, 3), (0,))
FIRST = (0, 1, 3)
PADDED = (48, 80, 48)


def kernel(
    count_ref, owner_ref, amp_ref, v_hbm, out_ref,
    raw, send0, send1, send2, got0, got1, got2, v_ref, perm, sel0, sel1, block, prod,
    far_out, far_in, near_out, near_in, far_out_s, far_in_s, near_out_s, near_in_s,
    v_sem, xs, xr, zs, zr, cs, cr, ys, yr, fs, fr, fas, far_, nes, ner, fass, fars, ness, ners,
):
    x = lax.axis_index("vir")
    o = lax.axis_index("occ")
    z, y, c = o // 8, (o // 2) % 4, o % 2
    yp, yl = y // 2, y % 2
    other = 3 - y
    partner = yp * 2 + 1 - yl
    sends = (send0, send1, send2)
    gots = (got0, got1, got2)

    def at(xx, zz, yy, cc):
        return (xx, (zz * 4 + yy) * 2 + cc)

    peers = [at((x + dx) % 4, z, y, (c + dc) % 2) for dx in range(4) for dc in range(2) if dx or dc]
    peers += [at(x, (z + dz) % 4, yy, c) for dz in range(4) for yy in (y, other) if dz or yy is other]
    peers += [at(x, z, partner, c)]
    barrier = pltpu.get_barrier_semaphore()
    for peer in peers:
        pl.semaphore_signal(barrier, inc=1, device_id=peer, device_id_type=MESH)

    v_copy = pltpu.make_async_copy(v_hbm, v_ref, v_sem.at[0])
    v_copy.start()
    pl.semaphore_wait(barrier, len(peers))

    order = (2, 1, 3, 0)

    def x_copy(place, dc):
        to = (x + 4 - order[place]) % 4
        cc = (c + dc) % 2
        src = amp_ref.at[:, pl.ds(pl.multiple_of(to * WIDE + cc * HALF, LANES), HALF)]
        dst = raw.at[pl.ds(pl.multiple_of((place * 2 + c) * BLOCK, 16), BLOCK), :]
        if order[place] == 0 and dc == 0:
            return pltpu.make_async_copy(src, dst, xr.at[place * 2])
        return pltpu.make_async_remote_copy(
            src_ref=src, dst_ref=dst, send_sem=xs.at[place * 2 + dc], recv_sem=xr.at[place * 2 + dc],
            device_id=at(to, z, y, cc), device_id_type=MESH,
        )

    def x_wait(place, dc):
        dst = raw.at[pl.ds(pl.multiple_of((place * 2 + (c + dc) % 2) * BLOCK, 16), BLOCK), :]
        pltpu.make_async_copy(dst, dst, xr.at[place * 2 + dc]).wait()

    for place in range(4):
        for dc in range(2):
            x_copy(place, dc).start()

    row = lax.broadcasted_iota(I32, (LANES, LANES), 0)
    col = lax.broadcasted_iota(I32, (LANES, LANES), 1)
    holds = jnp.zeros((LANES, LANES), I32)
    for g in range(SECTORS):
        holds = jnp.where((row >> 4) == g, owner_ref[g], holds)
    perm[...] = jnp.where(((row & 15) == (col >> 3)) & (holds == (col & 7)), 1.0, 0.0).astype(BF16)

    y_of = (2 * yp, 3 - 2 * yp, 2 * yp + 1, 2 - 2 * yp)
    for sel, padded, parts in ((sel0, PADDED[0], 1), (sel1, PADDED[1], 2)):
        for k in range(parts):
            out_row = lax.broadcasted_iota(I32, (ZBLOCK, 4 * padded), 0)
            in_row = lax.broadcasted_iota(I32, (ZBLOCK, 4 * padded), 1)
            base = jnp.zeros_like(in_row) + (y_of[0] * PAIR)
            inner = in_row - k * PAIR
            for j in range(1, 4):
                later = in_row >= j * padded
                base = jnp.where(later, y_of[j] * PAIR, base)
                inner = jnp.where(later, in_row - (j * padded + k * PAIR), inner)
            hit = (inner >= 0) & (inner < PAIR) & (out_row == base + inner)
            sel[k] = jnp.where(hit, 1.0, 0.0).astype(BF16)

    sector = owner_ref[o // 4]
    live = count_ref[sector] * TILE
    live_row = live - x * WIDE
    live_col = live - (o % 4) * WIDE
    v_copy.wait()

    def mask(i, _):
        rows = pl.ds(pl.multiple_of(i * 64, 64), 64)
        r = lax.broadcasted_iota(I32, (64, WIDE), 0) + i * 64
        k = lax.broadcasted_iota(I32, (64, WIDE), 1)
        m = jnp.where((r < live_row) & (k < live_col), 1.0, 0.0).astype(BF16)
        v_ref[rows, :] = v_ref[rows, :] * m
        return 0

    lax.fori_loop(0, WIDE // 64, mask, 0)

    half = pl.ds(pl.multiple_of(c * HALF, LANES), HALF)
    half_other = pl.ds(pl.multiple_of((1 - c) * HALF, LANES), HALF)

    def slot(ch, zz, yy, cols):
        padded = PADDED[ch]
        return gots[ch].at[pl.ds(pl.multiple_of((zz * 4 + yy) * padded, 16), padded), cols]

    def zy_copy(ch, dz, rp):
        padded = PADDED[ch]
        to_z = (z + dz) % 4
        to_y = other if rp else y
        g = to_z * 2 + to_y // 2
        src = sends[ch].at[pl.ds(pl.multiple_of(g * padded, 16), padded), :]
        dst = slot(ch, z, (to_y % 2) * 2 + rp, half)
        i = ch * 8 + dz * 2 + rp
        if dz == 0 and rp == 0:
            return pltpu.make_async_copy(src, dst, zr.at[i])
        return pltpu.make_async_remote_copy(
            src_ref=src, dst_ref=dst, send_sem=zs.at[i], recv_sem=zr.at[i],
            device_id=at(x, to_z, to_y, c), device_id_type=MESH,
        )

    def landed(ch, dz, rp, mine, cols):
        return slot(ch, (z + 4 - dz) % 4, (yl if mine else 1 - yl) * 2 + rp, cols)

    def wait_for(ref, sem):
        pltpu.make_async_copy(ref, ref, sem).wait()

    def pass_on(ch, dz, rp, kind):
        i = ch * 8 + dz * 2 + rp
        ref = landed(ch, dz, rp, kind != "f", half)
        ss, rr, device = {
            "c": (cs, cr, at(x, z, y, 1 - c)),
            "y": (ys, yr, at(x, z, partner, c)),
            "f": (fs, fr, at(x, z, y, 1 - c)),
        }[kind]
        return pltpu.make_async_remote_copy(
            src_ref=ref, dst_ref=ref, send_sem=ss.at[i], recv_sem=rr.at[i],
            device_id=device, device_id_type=MESH,
        )

    def choose(ch):
        padded = PADDED[ch]
        for k in range(len(CHUNKS[ch])):
            for dc in range(2):
                x_wait(FIRST[ch] + k, dc)
        rows = len(CHUNKS[ch]) * 2 * BLOCK
        start = FIRST[ch] * 2 * BLOCK
        for b in range(padded // 16):
            depth = min(LANES, rows - b * LANES)
            picked = jnp.dot(
                perm[:, :depth], raw[start + b * LANES : start + b * LANES + depth, :],
                preferred_element_type=F32,
            ).astype(BF16)
            for g in range(SECTORS):
                sends[ch][g * padded + 16 * b : g * padded + 16 * b + 16, :] = picked[16 * g : 16 * g + 16, :]
        for dz, rp in PLACES:
            zy_copy(ch, dz, rp).start()

    def spread(ch):
        for dz, rp in PLACES:
            wait_for(landed(ch, dz, rp, True, half), zr.at[ch * 8 + dz * 2 + rp])
            pass_on(ch, dz, rp, "y").start()
            pass_on(ch, dz, rp, "c").start()

    def forward(ch):
        for dz, rp in PLACES:
            wait_for(landed(ch, dz, rp, False, half), yr.at[ch * 8 + dz * 2 + rp])
            pass_on(ch, dz, rp, "f").start()

    def collect(ch):
        for dz, rp in PLACES:
            wait_for(landed(ch, dz, rp, True, half_other), cr.at[ch * 8 + dz * 2 + rp])
            wait_for(landed(ch, dz, rp, False, half_other), fr.at[ch * 8 + dz * 2 + rp])

    def multiply(ch, k, zz):
        padded = PADDED[ch]
        sel = (sel1 if ch == 1 else sel0).at[k]
        rows = pl.ds(pl.multiple_of(zz * 4 * padded, 16), 4 * padded)

        def pick(n, _):
            cols = pl.ds(pl.multiple_of(n * 256, 256), 256)
            block[:, cols] = jnp.dot(sel[...], gots[ch][rows, cols], preferred_element_type=F32).astype(BF16)
            return 0

        lax.fori_loop(0, WIDE // 256, pick, 0)

        def tile(n, _):
            cols = pl.ds(pl.multiple_of(n * 256, 256), 256)
            prod[:, cols] = jnp.dot(block[...], v_ref[:, cols], preferred_element_type=F32)
            return 0

        lax.fori_loop(0, WIDE // 256, tile, 0)

    def encode(codes, scale):
        def biggest(i, m):
            rows = pl.ds(pl.multiple_of(i * 16, 16), 16)
            for j in range(WIDE // LANES):
                m = jnp.maximum(m, jnp.abs(prod[rows, j * LANES : (j + 1) * LANES]))
            return m

        top = lax.fori_loop(0, ZBLOCK // 16, biggest, jnp.full((16, LANES), 1e-30, F32))
        scale[...] = top * (1.0 / TOP)
        inv = TOP / top

        def code(i, _):
            rows = pl.ds(pl.multiple_of(i * 16, 16), 16)
            for j in range(WIDE // LANES):
                cols = slice(j * LANES, (j + 1) * LANES)
                codes[rows, cols] = jnp.round(prod[rows, cols] * inv).astype(I32).astype(I16)
            return 0

        lax.fori_loop(0, ZBLOCK // 16, code, 0)

    def add(codes, scale):
        step = scale[...]

        def body(i, _):
            rows = pl.ds(pl.multiple_of(i * 16, 16), 16)
            for j in range(WIDE // LANES):
                cols = slice(j * LANES, (j + 1) * LANES)
                prod[rows, cols] += codes[rows, cols].astype(I32).astype(F32) * step
            return 0

        lax.fori_loop(0, ZBLOCK // 16, body, 0)

    def far_copies(zz):
        to = (x + 1 + 2 * (zz // 2)) % 4
        make = functools.partial(pltpu.make_async_remote_copy, device_id=at(to, z, y, c), device_id_type=MESH)
        return (
            make(src_ref=far_out.at[zz], dst_ref=far_in.at[zz], send_sem=fas.at[zz], recv_sem=far_.at[zz]),
            make(src_ref=far_out_s.at[zz], dst_ref=far_in_s.at[zz], send_sem=fass.at[zz], recv_sem=fars.at[zz]),
        )

    def near_copies(k, zz):
        to = (x + 1 + 2 * k) % 4
        i = k * 4 + zz
        make = functools.partial(pltpu.make_async_remote_copy, device_id=at(to, z, y, c), device_id_type=MESH)
        return (
            make(src_ref=near_out.at[i], dst_ref=near_in.at[i], send_sem=nes.at[i], recv_sem=ner.at[i]),
            make(src_ref=near_out_s.at[i], dst_ref=near_in_s.at[i], send_sem=ness.at[i], recv_sem=ners.at[i]),
        )

    def far_unit(i, _):
        zz = (i % 2) * 2 + i // 2
        multiply(0, 0, zz)
        encode(far_out.at[zz], far_out_s.at[zz])
        for copy in far_copies(zz):
            copy.start()
        return 0

    def near_unit(i, _):
        k = i % 2
        zz = 2 * (1 - k) + i // 2
        multiply(1, k, zz)
        encode(near_out.at[k * 4 + zz], near_out_s.at[k * 4 + zz])
        for copy in near_copies(k, zz):
            copy.start()
        return 0

    def joint_unit(i, _):
        k = i % 2
        zz = 2 * k + i // 2
        multiply(1, k, zz)
        wait_for(far_in.at[zz], far_.at[zz])
        wait_for(far_in_s.at[zz], fars.at[zz])
        add(far_in.at[zz], far_in_s.at[zz])
        encode(near_out.at[k * 4 + zz], near_out_s.at[k * 4 + zz])
        for copy in near_copies(k, zz):
            copy.start()
        return 0

    def last_unit(i, _):
        zz = (i % 2) * 2 + i // 2
        multiply(2, 0, zz)
        for k in range(2):
            j = k * 4 + zz
            wait_for(near_in.at[j], ner.at[j])
            wait_for(near_in_s.at[j], ners.at[j])
            add(near_in.at[j], near_in_s.at[j])
        rows = pl.ds(pl.multiple_of(zz * ZBLOCK, 16), ZBLOCK)
        out_ref[rows, :] = prod[...].astype(BF16)
        return 0

    choose(0)
    spread(0)
    choose(1)
    forward(0)
    spread(1)
    collect(0)
    lax.fori_loop(0, 4, far_unit, 0)
    choose(2)
    forward(1)
    collect(1)
    lax.fori_loop(0, 4, near_unit, 0)
    spread(2)
    lax.fori_loop(0, 4, joint_unit, 0)
    forward(2)
    collect(2)
    lax.fori_loop(0, 4, last_unit, 0)

    for place in range(4):
        for dc in range(2):
            if order[place] or dc:
                x_copy(place, dc).wait_send()
    for ch in range(3):
        for dz, rp in PLACES:
            if dz or rp:
                zy_copy(ch, dz, rp).wait_send()
            for kind in "cyf":
                pass_on(ch, dz, rp, kind).wait_send()

    def sent(i, _):
        for copy in far_copies(i):
            copy.wait_send()
        for k in range(2):
            for copy in near_copies(k, i):
                copy.wait_send()
        return 0

    lax.fori_loop(0, 4, sent, 0)


PLACES = ((0, 0), (0, 1), (1, 0), (3, 0), (1, 1), (3, 1), (2, 0), (2, 1))


def per_device(amplitudes, integrals, nonzero_tile_count, sector_owner):
    dma = pltpu.SemaphoreType.DMA
    vmem = pltpu.VMEM
    codes = [vmem((n, ZBLOCK, WIDE), I16) for n in (4, 4, 8, 8)]
    scales = [vmem((n, 16, LANES), F32) for n in (4, 4, 8, 8)]
    out = pl.pallas_call(
        kernel,
        out_shape=jax.ShapeDtypeStruct((4 * ZBLOCK, WIDE), BF16),
        in_specs=[
            pl.BlockSpec(memory_space=pltpu.SMEM),
            pl.BlockSpec(memory_space=pltpu.SMEM),
            pl.BlockSpec(memory_space=pl.ANY),
            pl.BlockSpec(memory_space=pl.ANY),
        ],
        out_specs=pl.BlockSpec(memory_space=pltpu.VMEM),
        scratch_shapes=[
            vmem((8 * BLOCK, HALF), BF16),
            *[vmem((SECTORS * p, HALF), BF16) for p in PADDED],
            *[vmem((16 * p, WIDE), BF16) for p in PADDED],
            vmem((WIDE, WIDE), BF16),
            vmem((LANES, LANES), BF16),
            vmem((1, ZBLOCK, 4 * PADDED[0]), BF16),
            vmem((2, ZBLOCK, 4 * PADDED[1]), BF16),
            vmem((ZBLOCK, WIDE), BF16),
            vmem((ZBLOCK, WIDE), F32),
            *codes,
            *scales,
            dma((1,)), dma((8,)), dma((8,)),
            *[dma((24,)) for _ in range(8)],
            dma((4,)), dma((4,)), dma((8,)), dma((8,)),
            dma((4,)), dma((4,)), dma((8,)), dma((8,)),
        ],
        compiler_params=pltpu.CompilerParams(
            collective_id=0, has_side_effects=True, vmem_limit_bytes=56 * 1024 * 1024
        ),
        cost_estimate=pl.CostEstimate(
            flops=2 * 16 * ZBLOCK * WIDE * WIDE, bytes_accessed=20_000_000, transcendentals=0
        ),
    )(
        nonzero_tile_count,
        sector_owner,
        amplitudes.reshape(BLOCK, amplitudes.shape[2]),
        integrals.reshape(WIDE, WIDE),
    )
    return out[:, None, :]


def solution(mesh):
    in_specs = (P(("vir", "occ"), None, None), P("occ", "vir", None), P(), P())
    out_specs = P("vir", "occ", None)
    return jax.shard_map(
        per_device, mesh=mesh, in_specs=in_specs, out_specs=out_specs, check_vma=False
    )
```

```python
import functools

import jax
import jax.numpy as jnp
from jax import lax
from jax.experimental import pallas as pl
from jax.experimental.pallas import tpu as pltpu
from jax.sharding import PartitionSpec as P

TILE = 64
MESH = pl.DeviceIdType.MESH
F32, BF16, I16, I32 = jnp.float32, jnp.bfloat16, jnp.int16, jnp.int32

ROWS = 18
SECTORS = 8
PAIR = 2 * ROWS
ZBLOCK = 4 * PAIR
HALF = 896
WIDE = 1792
LANES = 128
BLOCK = ROWS * SECTORS
TOP = 32752.0

CHUNKS = ((2,), (1, 3), (0,))
FIRST = (0, 1, 3)
PADDED = (48, 80, 48)


def kernel(
    count_ref, owner_ref, amp_ref, v_hbm, out_ref,
    raw, send0, send1, send2, got0, got1, got2, v_ref, perm, wide, prod,
    far_out, far_in, near_out, near_in, far_out_s, far_in_s, near_out_s, near_in_s,
    v_sem, xs, xr, zs, zr, cs, cr, ys, yr, fs, fr, fas, far_, nes, ner, fass, fars, ness, ners,
):
    x = lax.axis_index("vir")
    o = lax.axis_index("occ")
    z, y, c = o // 8, (o // 2) % 4, o % 2
    yp, yl = y // 2, y % 2
    other = 3 - y
    partner = yp * 2 + 1 - yl
    sends = (send0, send1, send2)
    gots = (got0, got1, got2)

    def at(xx, zz, yy, cc):
        return (xx, (zz * 4 + yy) * 2 + cc)

    peers = [at((x + dx) % 4, z, y, (c + dc) % 2) for dx in range(4) for dc in range(2) if dx or dc]
    peers += [at(x, (z + dz) % 4, yy, c) for dz in range(4) for yy in (y, other) if dz or yy is other]
    peers += [at(x, z, partner, c)]
    barrier = pltpu.get_barrier_semaphore()
    for peer in peers:
        pl.semaphore_signal(barrier, inc=1, device_id=peer, device_id_type=MESH)

    v_copy = pltpu.make_async_copy(v_hbm, v_ref, v_sem.at[0])
    v_copy.start()
    pl.semaphore_wait(barrier, len(peers))

    order = (2, 1, 3, 0)

    def x_copy(place, dc):
        to = (x + 4 - order[place]) % 4
        cc = (c + dc) % 2
        src = amp_ref.at[:, pl.ds(pl.multiple_of(to * WIDE + cc * HALF, LANES), HALF)]
        dst = raw.at[pl.ds(pl.multiple_of((place * 2 + c) * BLOCK, 16), BLOCK), :]
        if order[place] == 0 and dc == 0:
            return pltpu.make_async_copy(src, dst, xr.at[place * 2])
        return pltpu.make_async_remote_copy(
            src_ref=src, dst_ref=dst, send_sem=xs.at[place * 2 + dc], recv_sem=xr.at[place * 2 + dc],
            device_id=at(to, z, y, cc), device_id_type=MESH,
        )

    def x_wait(place, dc):
        dst = raw.at[pl.ds(pl.multiple_of((place * 2 + (c + dc) % 2) * BLOCK, 16), BLOCK), :]
        pltpu.make_async_copy(dst, dst, xr.at[place * 2 + dc]).wait()

    for place in range(4):
        for dc in range(2):
            x_copy(place, dc).start()

    row = lax.broadcasted_iota(I32, (LANES, LANES), 0)
    col = lax.broadcasted_iota(I32, (LANES, LANES), 1)
    holds = jnp.zeros((LANES, LANES), I32)
    for g in range(SECTORS):
        holds = jnp.where((row >> 4) == g, owner_ref[g], holds)
    perm[...] = jnp.where(((row & 15) == (col >> 3)) & (holds == (col & 7)), 1.0, 0.0).astype(BF16)

    sector = owner_ref[o // 4]
    live = count_ref[sector] * TILE
    live_row = live - x * WIDE
    live_col = live - (o % 4) * WIDE
    v_copy.wait()

    def mask(i, _):
        rows = pl.ds(pl.multiple_of(i * 64, 64), 64)
        r = lax.broadcasted_iota(I32, (64, WIDE), 0) + i * 64
        k = lax.broadcasted_iota(I32, (64, WIDE), 1)
        m = jnp.where((r < live_row) & (k < live_col), 1.0, 0.0).astype(BF16)
        v_ref[rows, :] = v_ref[rows, :] * m
        return 0

    lax.fori_loop(0, WIDE // 64, mask, 0)

    half = pl.ds(pl.multiple_of(c * HALF, LANES), HALF)
    half_other = pl.ds(pl.multiple_of((1 - c) * HALF, LANES), HALF)

    def slot(ch, zz, yy, cols):
        padded = PADDED[ch]
        return gots[ch].at[pl.ds(pl.multiple_of((zz * 4 + yy) * padded, 16), padded), cols]

    def zy_copy(ch, dz, rp):
        padded = PADDED[ch]
        to_z = (z + dz) % 4
        to_y = other if rp else y
        g = to_z * 2 + to_y // 2
        src = sends[ch].at[pl.ds(pl.multiple_of(g * padded, 16), padded), :]
        dst = slot(ch, z, (to_y % 2) * 2 + rp, half)
        i = ch * 8 + dz * 2 + rp
        if dz == 0 and rp == 0:
            return pltpu.make_async_copy(src, dst, zr.at[i])
        return pltpu.make_async_remote_copy(
            src_ref=src, dst_ref=dst, send_sem=zs.at[i], recv_sem=zr.at[i],
            device_id=at(x, to_z, to_y, c), device_id_type=MESH,
        )

    def landed(ch, dz, rp, mine, cols):
        return slot(ch, (z + 4 - dz) % 4, (yl if mine else 1 - yl) * 2 + rp, cols)

    def wait_for(ref, sem):
        pltpu.make_async_copy(ref, ref, sem).wait()

    def pass_on(ch, dz, rp, kind):
        i = ch * 8 + dz * 2 + rp
        ref = landed(ch, dz, rp, kind != "f", half)
        ss, rr, device = {
            "c": (cs, cr, at(x, z, y, 1 - c)),
            "y": (ys, yr, at(x, z, partner, c)),
            "f": (fs, fr, at(x, z, y, 1 - c)),
        }[kind]
        return pltpu.make_async_remote_copy(
            src_ref=ref, dst_ref=ref, send_sem=ss.at[i], recv_sem=rr.at[i],
            device_id=device, device_id_type=MESH,
        )

    def choose(ch):
        padded = PADDED[ch]
        for k in range(len(CHUNKS[ch])):
            for dc in range(2):
                x_wait(FIRST[ch] + k, dc)
        rows = len(CHUNKS[ch]) * 2 * BLOCK
        start = FIRST[ch] * 2 * BLOCK
        for b in range(padded // 16):
            depth = min(LANES, rows - b * LANES)
            picked = jnp.dot(
                perm[:, :depth], raw[start + b * LANES : start + b * LANES + depth, :],
                preferred_element_type=F32,
            ).astype(BF16)
            for g in range(SECTORS):
                sends[ch][g * padded + 16 * b : g * padded + 16 * b + 16, :] = picked[16 * g : 16 * g + 16, :]
        for dz, rp in PLACES:
            zy_copy(ch, dz, rp).start()

    def spread(ch, dz):
        for rp in range(2):
            wait_for(landed(ch, dz, rp, True, half), zr.at[ch * 8 + dz * 2 + rp])
            pass_on(ch, dz, rp, "y").start()
            pass_on(ch, dz, rp, "c").start()

    def forward(ch, dz):
        for rp in range(2):
            wait_for(landed(ch, dz, rp, False, half), yr.at[ch * 8 + dz * 2 + rp])
            pass_on(ch, dz, rp, "f").start()

    def collect(ch, dz):
        for rp in range(2):
            wait_for(landed(ch, dz, rp, True, half_other), cr.at[ch * 8 + dz * 2 + rp])
            wait_for(landed(ch, dz, rp, False, half_other), fr.at[ch * 8 + dz * 2 + rp])

    def multiply(ch, dz):
        height = 4 * PADDED[ch]
        rows = pl.ds(pl.multiple_of((z + 4 - dz) % 4 * height, 16), height)
        wide[:height, :] = jnp.dot(gots[ch][rows, :], v_ref[...], preferred_element_type=F32)

    def compact(ch, k):
        for side in range(2):
            for part in range(len(CHUNKS[ch])):

                @pl.when((yp == side) & (k == part))
                def _():
                    for j in range(4):
                        to = Y_OF[side][j] * PAIR
                        start = j * PADDED[ch] + part * PAIR
                        prod[to : to + PAIR, :] = wide[start : start + PAIR, :]

    def encode(codes, scale):
        def biggest(i, m):
            rows = pl.ds(pl.multiple_of(i * 16, 16), 16)
            for j in range(WIDE // LANES):
                m = jnp.maximum(m, jnp.abs(prod[rows, j * LANES : (j + 1) * LANES]))
            return m

        top = lax.fori_loop(0, ZBLOCK // 16, biggest, jnp.full((16, LANES), 1e-30, F32))
        scale[...] = top * (1.0 / TOP)
        inv = TOP / top

        def code(i, _):
            rows = pl.ds(pl.multiple_of(i * 16, 16), 16)
            for j in range(WIDE // LANES):
                cols = slice(j * LANES, (j + 1) * LANES)
                codes[rows, cols] = jnp.round(prod[rows, cols] * inv).astype(I32).astype(I16)
            return 0

        lax.fori_loop(0, ZBLOCK // 16, code, 0)

    def add(codes, scale):
        step = scale[...]

        def body(i, _):
            rows = pl.ds(pl.multiple_of(i * 16, 16), 16)
            for j in range(WIDE // LANES):
                cols = slice(j * LANES, (j + 1) * LANES)
                prod[rows, cols] += codes[rows, cols].astype(I32).astype(F32) * step
            return 0

        lax.fori_loop(0, ZBLOCK // 16, body, 0)

    def far_copies(i):
        to = (x + 1 + 2 * (i % 2)) % 4
        make = functools.partial(pltpu.make_async_remote_copy, device_id=at(to, z, y, c), device_id_type=MESH)
        return (
            make(src_ref=far_out.at[i], dst_ref=far_in.at[i], send_sem=fas.at[i], recv_sem=far_.at[i]),
            make(src_ref=far_out_s.at[i], dst_ref=far_in_s.at[i], send_sem=fass.at[i], recv_sem=fars.at[i]),
        )

    def near_copies(k, i):
        to = (x + 1 + 2 * k) % 4
        j = k * 4 + i
        make = functools.partial(pltpu.make_async_remote_copy, device_id=at(to, z, y, c), device_id_type=MESH)
        return (
            make(src_ref=near_out.at[j], dst_ref=near_in.at[j], send_sem=nes.at[j], recv_sem=ner.at[j]),
            make(src_ref=near_out_s.at[j], dst_ref=near_in_s.at[j], send_sem=ness.at[j], recv_sem=ners.at[j]),
        )

    def far_step(i, _):
        dz = i + i // 2 - 2 * (i // 3)
        forward(0, dz)
        collect(0, dz)
        multiply(0, dz)
        compact(0, 0)
        encode(far_out.at[i], far_out_s.at[i])
        for copy in far_copies(i):
            copy.start()

        @pl.when(i == 0)
        def _():
            choose(1)

        spread(1, dz)
        return 0

    def near_step(i, _):
        dz = i + i // 2 - 2 * (i // 3)
        forward(1, dz)
        collect(1, dz)
        multiply(1, dz)
        joint = i % 2
        alone = 1 - joint
        compact(1, alone)
        encode(near_out.at[alone * 4 + i], near_out_s.at[alone * 4 + i])
        for copy in near_copies(alone, i):
            copy.start()
        compact(1, joint)
        wait_for(far_in.at[i], far_.at[i])
        wait_for(far_in_s.at[i], fars.at[i])
        add(far_in.at[i], far_in_s.at[i])
        encode(near_out.at[joint * 4 + i], near_out_s.at[joint * 4 + i])
        for copy in near_copies(joint, i):
            copy.start()

        @pl.when(i == 0)
        def _():
            choose(2)

        spread(2, dz)
        return 0

    def last_step(i, _):
        dz = i + i // 2 - 2 * (i // 3)
        forward(2, dz)
        collect(2, dz)
        multiply(2, dz)
        compact(2, 0)
        for k in range(2):
            j = k * 4 + i
            wait_for(near_in.at[j], ner.at[j])
            wait_for(near_in_s.at[j], ners.at[j])
            add(near_in.at[j], near_in_s.at[j])
        rows = pl.ds(pl.multiple_of((z + 4 - dz) % 4 * ZBLOCK, 16), ZBLOCK)
        out_ref[rows, :] = prod[...].astype(BF16)
        return 0

    choose(0)
    for dz in (0, 1, 3, 2):
        spread(0, dz)
    lax.fori_loop(0, 4, far_step, 0)
    lax.fori_loop(0, 4, near_step, 0)
    lax.fori_loop(0, 4, last_step, 0)

    for place in range(4):
        for dc in range(2):
            if order[place] or dc:
                x_copy(place, dc).wait_send()
    for ch in range(3):
        for dz, rp in PLACES:
            if dz or rp:
                zy_copy(ch, dz, rp).wait_send()
            for kind in "cyf":
                pass_on(ch, dz, rp, kind).wait_send()

    def sent(i, _):
        for copy in far_copies(i):
            copy.wait_send()
        for k in range(2):
            for copy in near_copies(k, i):
                copy.wait_send()
        return 0

    lax.fori_loop(0, 4, sent, 0)


Y_OF = ((0, 3, 1, 2), (2, 1, 3, 0))
PLACES = ((0, 0), (0, 1), (1, 0), (3, 0), (1, 1), (3, 1), (2, 0), (2, 1))


def per_device(amplitudes, integrals, nonzero_tile_count, sector_owner):
    dma = pltpu.SemaphoreType.DMA
    vmem = pltpu.VMEM
    codes = [vmem((n, ZBLOCK, WIDE), I16) for n in (4, 4, 8, 8)]
    scales = [vmem((n, 16, LANES), F32) for n in (4, 4, 8, 8)]
    out = pl.pallas_call(
        kernel,
        out_shape=jax.ShapeDtypeStruct((4 * ZBLOCK, WIDE), BF16),
        in_specs=[
            pl.BlockSpec(memory_space=pltpu.SMEM),
            pl.BlockSpec(memory_space=pltpu.SMEM),
            pl.BlockSpec(memory_space=pl.ANY),
            pl.BlockSpec(memory_space=pl.ANY),
        ],
        out_specs=pl.BlockSpec(memory_space=pltpu.VMEM),
        scratch_shapes=[
            vmem((8 * BLOCK, HALF), BF16),
            *[vmem((SECTORS * p, HALF), BF16) for p in PADDED],
            *[vmem((16 * p, WIDE), BF16) for p in PADDED],
            vmem((WIDE, WIDE), BF16),
            vmem((LANES, LANES), BF16),
            vmem((4 * max(PADDED), WIDE), F32),
            vmem((ZBLOCK, WIDE), F32),
            *codes,
            *scales,
            dma((1,)), dma((8,)), dma((8,)),
            *[dma((24,)) for _ in range(8)],
            dma((4,)), dma((4,)), dma((8,)), dma((8,)),
            dma((4,)), dma((4,)), dma((8,)), dma((8,)),
        ],
        compiler_params=pltpu.CompilerParams(
            collective_id=0, has_side_effects=True, vmem_limit_bytes=56 * 1024 * 1024
        ),
        cost_estimate=pl.CostEstimate(
            flops=2 * 16 * ZBLOCK * WIDE * WIDE, bytes_accessed=20_000_000, transcendentals=0
        ),
    )(
        nonzero_tile_count,
        sector_owner,
        amplitudes.reshape(BLOCK, amplitudes.shape[2]),
        integrals.reshape(WIDE, WIDE),
    )
    return out[:, None, :]


def solution(mesh):
    in_specs = (P(("vir", "occ"), None, None), P("occ", "vir", None), P(), P())
    out_specs = P("vir", "occ", None)
    return jax.shard_map(
        per_device, mesh=mesh, in_specs=in_specs, out_specs=out_specs, check_vma=False
    )
```

```python
import functools

import jax
import jax.numpy as jnp
from jax import lax
from jax.experimental import pallas as pl
from jax.experimental.pallas import tpu as pltpu
from jax.sharding import PartitionSpec as P

TILE = 64
MESH = pl.DeviceIdType.MESH
F32, BF16, I16, I32 = jnp.float32, jnp.bfloat16, jnp.int16, jnp.int32

ROWS = 18
SECTORS = 8
PAIR = 2 * ROWS
ZBLOCK = 4 * PAIR
HALF = 896
WIDE = 1792
LANES = 128
BLOCK = ROWS * SECTORS
TOP = 32752.0

CHUNKS = ((2,), (1, 3), (0,))
FIRST = (0, 1, 3)
PADDED = (48, 80, 48)


def kernel(
    count_ref, owner_ref, amp_ref, v_hbm, out_ref,
    raw, send0, send1, send2, got0, got1, got2, v_ref, perm, wide, prod, done, out_sem,
    far_out, far_in, near_out, near_in, far_out_s, far_in_s, near_out_s, near_in_s,
    v_sem, xs, xr, zs, zr, cs, cr, ys, yr, fs, fr, fas, far_, nes, ner, fass, fars, ness, ners,
):
    x = lax.axis_index("vir")
    o = lax.axis_index("occ")
    z, y, c = o // 8, (o // 2) % 4, o % 2
    yp, yl = y // 2, y % 2
    other = 3 - y
    partner = yp * 2 + 1 - yl
    sends = (send0, send1, send2)
    gots = (got0, got1, got2)

    def at(xx, zz, yy, cc):
        return (xx, (zz * 4 + yy) * 2 + cc)

    peers = [at((x + dx) % 4, z, y, (c + dc) % 2) for dx in range(4) for dc in range(2) if dx or dc]
    peers += [at(x, (z + dz) % 4, yy, c) for dz in range(4) for yy in (y, other) if dz or yy is other]
    peers += [at(x, z, partner, c)]
    barrier = pltpu.get_barrier_semaphore()
    for peer in peers:
        pl.semaphore_signal(barrier, inc=1, device_id=peer, device_id_type=MESH)

    v_copy = pltpu.make_async_copy(v_hbm, v_ref, v_sem.at[0])
    v_copy.start()
    pl.semaphore_wait(barrier, len(peers))

    order = (2, 1, 3, 0)

    def x_copy(place, dc):
        to = (x + 4 - order[place]) % 4
        cc = (c + dc) % 2
        src = amp_ref.at[:, pl.ds(pl.multiple_of(to * WIDE + cc * HALF, LANES), HALF)]
        dst = raw.at[pl.ds(pl.multiple_of((place * 2 + c) * BLOCK, 16), BLOCK), :]
        if order[place] == 0 and dc == 0:
            return pltpu.make_async_copy(src, dst, xr.at[place * 2])
        return pltpu.make_async_remote_copy(
            src_ref=src, dst_ref=dst, send_sem=xs.at[place * 2 + dc], recv_sem=xr.at[place * 2 + dc],
            device_id=at(to, z, y, cc), device_id_type=MESH,
        )

    def x_wait(place, dc):
        dst = raw.at[pl.ds(pl.multiple_of((place * 2 + (c + dc) % 2) * BLOCK, 16), BLOCK), :]
        pltpu.make_async_copy(dst, dst, xr.at[place * 2 + dc]).wait()

    for dc in range(2):
        x_copy(0, dc).start()

    row = lax.broadcasted_iota(I32, (LANES, LANES), 0)
    col = lax.broadcasted_iota(I32, (LANES, LANES), 1)
    holds = jnp.zeros((LANES, LANES), I32)
    for g in range(SECTORS):
        holds = jnp.where((row >> 4) == g, owner_ref[g], holds)
    perm[...] = jnp.where(((row & 15) == (col >> 3)) & (holds == (col & 7)), 1.0, 0.0).astype(BF16)

    sector = owner_ref[o // 4]
    live = count_ref[sector] * TILE
    live_row = live - x * WIDE
    live_col = live - (o % 4) * WIDE
    v_copy.wait()

    def mask(i, _):
        rows = pl.ds(pl.multiple_of(i * 64, 64), 64)
        r = lax.broadcasted_iota(I32, (64, WIDE), 0) + i * 64
        k = lax.broadcasted_iota(I32, (64, WIDE), 1)
        m = jnp.where((r < live_row) & (k < live_col), 1.0, 0.0).astype(BF16)
        v_ref[rows, :] = v_ref[rows, :] * m
        return 0

    lax.fori_loop(0, WIDE // 64, mask, 0)

    half = pl.ds(pl.multiple_of(c * HALF, LANES), HALF)
    half_other = pl.ds(pl.multiple_of((1 - c) * HALF, LANES), HALF)

    def slot(ch, zz, yy, cols):
        padded = PADDED[ch]
        return gots[ch].at[pl.ds(pl.multiple_of((zz * 4 + yy) * padded, 16), padded), cols]

    def zy_copy(ch, dz, rp):
        padded = PADDED[ch]
        to_z = (z + dz) % 4
        to_y = other if rp else y
        g = to_z * 2 + to_y // 2
        src = sends[ch].at[pl.ds(pl.multiple_of(g * padded, 16), padded), :]
        dst = slot(ch, z, (to_y % 2) * 2 + rp, half)
        i = ch * 8 + dz * 2 + rp
        if dz == 0 and rp == 0:
            return pltpu.make_async_copy(src, dst, zr.at[i])
        return pltpu.make_async_remote_copy(
            src_ref=src, dst_ref=dst, send_sem=zs.at[i], recv_sem=zr.at[i],
            device_id=at(x, to_z, to_y, c), device_id_type=MESH,
        )

    def landed(ch, dz, rp, mine, cols):
        return slot(ch, (z + 4 - dz) % 4, (yl if mine else 1 - yl) * 2 + rp, cols)

    def wait_for(ref, sem):
        pltpu.make_async_copy(ref, ref, sem).wait()

    def pass_on(ch, dz, rp, kind):
        i = ch * 8 + dz * 2 + rp
        ref = landed(ch, dz, rp, kind != "f", half)
        ss, rr, device = {
            "c": (cs, cr, at(x, z, y, 1 - c)),
            "y": (ys, yr, at(x, z, partner, c)),
            "f": (fs, fr, at(x, z, y, 1 - c)),
        }[kind]
        return pltpu.make_async_remote_copy(
            src_ref=ref, dst_ref=ref, send_sem=ss.at[i], recv_sem=rr.at[i],
            device_id=device, device_id_type=MESH,
        )

    def choose(ch):
        padded = PADDED[ch]
        for k in range(len(CHUNKS[ch])):
            for dc in range(2):
                x_wait(FIRST[ch] + k, dc)
        if ch == 0:
            for place in (1, 2, 3):
                for dc in range(2):
                    x_copy(place, dc).start()
        rows = len(CHUNKS[ch]) * 2 * BLOCK
        start = FIRST[ch] * 2 * BLOCK
        for b in range(padded // 16):
            depth = min(LANES, rows - b * LANES)
            picked = jnp.dot(
                perm[:, :depth], raw[start + b * LANES : start + b * LANES + depth, :],
                preferred_element_type=F32,
            ).astype(BF16)
            for g in range(SECTORS):
                sends[ch][g * padded + 16 * b : g * padded + 16 * b + 16, :] = picked[16 * g : 16 * g + 16, :]
        for dz, rp in PLACES:
            zy_copy(ch, dz, rp).start()

    def spread(ch, dz):
        for rp in range(2):
            wait_for(landed(ch, dz, rp, True, half), zr.at[ch * 8 + dz * 2 + rp])
            pass_on(ch, dz, rp, "y").start()
            pass_on(ch, dz, rp, "c").start()

    def forward(ch, dz):
        for rp in range(2):
            wait_for(landed(ch, dz, rp, False, half), yr.at[ch * 8 + dz * 2 + rp])
            pass_on(ch, dz, rp, "f").start()

    def collect(ch, dz):
        for rp in range(2):
            wait_for(landed(ch, dz, rp, True, half_other), cr.at[ch * 8 + dz * 2 + rp])
            wait_for(landed(ch, dz, rp, False, half_other), fr.at[ch * 8 + dz * 2 + rp])

    def multiply(ch, dz):
        height = 4 * PADDED[ch]
        rows = pl.ds(pl.multiple_of((z + 4 - dz) % 4 * height, 16), height)
        wide[:height, :] = jnp.dot(gots[ch][rows, :], v_ref[...], preferred_element_type=F32)

    def compact(ch, k):
        for side in range(2):
            for part in range(len(CHUNKS[ch])):

                @pl.when((yp == side) & (k == part))
                def _():
                    for j in range(4):
                        to = Y_OF[side][j] * PAIR
                        start = j * PADDED[ch] + part * PAIR
                        prod[to : to + PAIR, :] = wide[start : start + PAIR, :]

    def encode(codes, scale):
        def biggest(i, m):
            rows = pl.ds(pl.multiple_of(i * 16, 16), 16)
            for j in range(WIDE // LANES):
                m = jnp.maximum(m, jnp.abs(prod[rows, j * LANES : (j + 1) * LANES]))
            return m

        top = lax.fori_loop(0, ZBLOCK // 16, biggest, jnp.full((16, LANES), 1e-30, F32))
        scale[...] = top * (1.0 / TOP)
        inv = TOP / top

        def code(i, _):
            rows = pl.ds(pl.multiple_of(i * 16, 16), 16)
            for j in range(WIDE // LANES):
                cols = slice(j * LANES, (j + 1) * LANES)
                codes[rows, cols] = jnp.round(prod[rows, cols] * inv).astype(I32).astype(I16)
            return 0

        lax.fori_loop(0, ZBLOCK // 16, code, 0)

    def add(codes, scale):
        step = scale[...]

        def body(i, _):
            rows = pl.ds(pl.multiple_of(i * 16, 16), 16)
            for j in range(WIDE // LANES):
                cols = slice(j * LANES, (j + 1) * LANES)
                prod[rows, cols] += codes[rows, cols].astype(I32).astype(F32) * step
            return 0

        lax.fori_loop(0, ZBLOCK // 16, body, 0)

    def far_copies(i):
        to = (x + 1 + 2 * (i % 2)) % 4
        make = functools.partial(pltpu.make_async_remote_copy, device_id=at(to, z, y, c), device_id_type=MESH)
        return (
            make(src_ref=far_out.at[i], dst_ref=far_in.at[i], send_sem=fas.at[i], recv_sem=far_.at[i]),
            make(src_ref=far_out_s.at[i], dst_ref=far_in_s.at[i], send_sem=fass.at[i], recv_sem=fars.at[i]),
        )

    def near_copies(k, i):
        to = (x + 1 + 2 * k) % 4
        j = k * 4 + i
        make = functools.partial(pltpu.make_async_remote_copy, device_id=at(to, z, y, c), device_id_type=MESH)
        return (
            make(src_ref=near_out.at[j], dst_ref=near_in.at[j], send_sem=nes.at[j], recv_sem=ner.at[j]),
            make(src_ref=near_out_s.at[j], dst_ref=near_in_s.at[j], send_sem=ness.at[j], recv_sem=ners.at[j]),
        )

    def plane(i):
        return i + i // 2 - 2 * (i // 3)

    def far_step(i, _):
        dz = plane(i)

        @pl.when(i < 3)
        def _():
            spread(0, plane(i + 1))

        forward(0, dz)
        collect(0, dz)
        multiply(0, dz)
        compact(0, 0)
        encode(far_out.at[i], far_out_s.at[i])
        for copy in far_copies(i):
            copy.start()

        @pl.when(i == 1)
        def _():
            choose(1)

        @pl.when(i >= 2)
        def _():
            spread(1, plane(i - 2))

        return 0

    def near_step(i, _):
        dz = plane(i)

        @pl.when(i < 2)
        def _():
            spread(1, plane(i + 2))

        forward(1, dz)
        collect(1, dz)
        multiply(1, dz)
        joint = i % 2
        alone = 1 - joint
        compact(1, alone)
        encode(near_out.at[alone * 4 + i], near_out_s.at[alone * 4 + i])
        for copy in near_copies(alone, i):
            copy.start()
        compact(1, joint)
        wait_for(far_in.at[i], far_.at[i])
        wait_for(far_in_s.at[i], fars.at[i])
        add(far_in.at[i], far_in_s.at[i])
        encode(near_out.at[joint * 4 + i], near_out_s.at[joint * 4 + i])
        for copy in near_copies(joint, i):
            copy.start()

        @pl.when(i == 0)
        def _():
            choose(2)

        @pl.when(i >= 1)
        def _():
            spread(2, plane(i - 1))

        return 0

    def out_copy(i):
        rows = pl.ds(pl.multiple_of((z + 4 - plane(i)) % 4 * ZBLOCK, 16), ZBLOCK)
        return pltpu.make_async_copy(done.at[i], out_ref.at[rows, :], out_sem.at[i])

    def last_step(i, _):
        dz = plane(i)

        @pl.when(i == 0)
        def _():
            spread(2, plane(3))

        forward(2, dz)
        collect(2, dz)
        multiply(2, dz)
        compact(2, 0)
        for k in range(2):
            j = k * 4 + i
            wait_for(near_in.at[j], ner.at[j])
            wait_for(near_in_s.at[j], ners.at[j])
            add(near_in.at[j], near_in_s.at[j])
        done[i] = prod[...].astype(BF16)
        out_copy(i).start()
        return 0

    choose(0)
    spread(0, 0)
    lax.fori_loop(0, 4, far_step, 0)
    lax.fori_loop(0, 4, near_step, 0)
    lax.fori_loop(0, 4, last_step, 0)

    for place in range(4):
        for dc in range(2):
            if order[place] or dc:
                x_copy(place, dc).wait_send()
    for ch in range(3):
        for dz, rp in PLACES:
            if dz or rp:
                zy_copy(ch, dz, rp).wait_send()
            for kind in "cyf":
                pass_on(ch, dz, rp, kind).wait_send()

    def sent(i, _):
        for copy in far_copies(i):
            copy.wait_send()
        for k in range(2):
            for copy in near_copies(k, i):
                copy.wait_send()
        out_copy(i).wait()
        return 0

    lax.fori_loop(0, 4, sent, 0)


Y_OF = ((0, 3, 1, 2), (2, 1, 3, 0))
PLACES = ((0, 0), (0, 1), (1, 0), (3, 0), (1, 1), (3, 1), (2, 0), (2, 1))


def per_device(amplitudes, integrals, nonzero_tile_count, sector_owner):
    dma = pltpu.SemaphoreType.DMA
    vmem = pltpu.VMEM
    codes = [vmem((n, ZBLOCK, WIDE), I16) for n in (4, 4, 8, 8)]
    scales = [vmem((n, 16, LANES), F32) for n in (4, 4, 8, 8)]
    out = pl.pallas_call(
        kernel,
        out_shape=jax.ShapeDtypeStruct((4 * ZBLOCK, WIDE), BF16),
        in_specs=[
            pl.BlockSpec(memory_space=pltpu.SMEM),
            pl.BlockSpec(memory_space=pltpu.SMEM),
            pl.BlockSpec(memory_space=pltpu.HBM),
            pl.BlockSpec(memory_space=pltpu.HBM),
        ],
        out_specs=pl.BlockSpec(memory_space=pl.ANY),
        scratch_shapes=[
            vmem((8 * BLOCK, HALF), BF16),
            *[vmem((SECTORS * p, HALF), BF16) for p in PADDED],
            *[vmem((16 * p, WIDE), BF16) for p in PADDED],
            vmem((WIDE, WIDE), BF16),
            vmem((LANES, LANES), BF16),
            vmem((4 * max(PADDED), WIDE), F32),
            vmem((ZBLOCK, WIDE), F32),
            vmem((4, ZBLOCK, WIDE), BF16),
            dma((4,)),
            *codes,
            *scales,
            dma((1,)), dma((8,)), dma((8,)),
            *[dma((24,)) for _ in range(8)],
            dma((4,)), dma((4,)), dma((8,)), dma((8,)),
            dma((4,)), dma((4,)), dma((8,)), dma((8,)),
        ],
        compiler_params=pltpu.CompilerParams(
            collective_id=0, has_side_effects=True, vmem_limit_bytes=51 * 1024 * 1024
        ),
        cost_estimate=pl.CostEstimate(
            flops=2 * 16 * ZBLOCK * WIDE * WIDE, bytes_accessed=20_000_000, transcendentals=0
        ),
    )(
        nonzero_tile_count,
        sector_owner,
        amplitudes.reshape(BLOCK, amplitudes.shape[2]),
        integrals.reshape(WIDE, WIDE),
    )
    return out[:, None, :]


def solution(mesh):
    in_specs = (P(("vir", "occ"), None, None), P("occ", "vir", None), P(), P())
    out_specs = P("vir", "occ", None)
    return jax.shard_map(
        per_device, mesh=mesh, in_specs=in_specs, out_specs=out_specs, check_vma=False
    )
```

```python
import functools

import jax
import jax.numpy as jnp
from jax import lax
from jax.experimental import pallas as pl
from jax.experimental.pallas import tpu as pltpu
from jax.sharding import PartitionSpec as P

TILE = 64
MESH = pl.DeviceIdType.MESH
F32, BF16, I16, I32 = jnp.float32, jnp.bfloat16, jnp.int16, jnp.int32

ROWS = 18
SECTORS = 8
PAIR = 2 * ROWS
ZBLOCK = 4 * PAIR
HALF = 896
WIDE = 1792
LANES = 128
BLOCK = ROWS * SECTORS
TOP = 32752.0

CHUNKS = ((2,), (1, 3), (0,))
FIRST = (0, 1, 3)
PADDED = (48, 80, 48)


def kernel(
    count_hbm, owner_hbm, amp_ref, v_hbm, out_ref,
    count_ref, owner_ref, int_sem,
    raw, send0, send1, send2, got0, got1, got2, v_ref, perm, wide, prod, done, out_sem,
    far_out, far_in, near_out, near_in, far_out_s, far_in_s, near_out_s, near_in_s,
    v_sem, xs, xr, zs, zr, cs, cr, ys, yr, fs, fr, fas, far_, nes, ner, fass, fars, ness, ners,
):
    x = lax.axis_index("vir")
    o = lax.axis_index("occ")
    z, y, c = o // 8, (o // 2) % 4, o % 2
    yp, yl = y // 2, y % 2
    other = 3 - y
    partner = yp * 2 + 1 - yl
    sends = (send0, send1, send2)
    gots = (got0, got1, got2)

    def at(xx, zz, yy, cc):
        return (xx, (zz * 4 + yy) * 2 + cc)

    peers = [at((x + dx) % 4, z, y, (c + dc) % 2) for dx in range(4) for dc in range(2) if dx or dc]
    peers += [at(x, (z + dz) % 4, yy, c) for dz in range(4) for yy in (y, other) if dz or yy is other]
    peers += [at(x, z, partner, c)]
    barrier = pltpu.get_barrier_semaphore()
    for peer in peers:
        pl.semaphore_signal(barrier, inc=1, device_id=peer, device_id_type=MESH)

    v_copy = pltpu.make_async_copy(v_hbm, v_ref, v_sem.at[0])
    v_copy.start()
    count_copy = pltpu.make_async_copy(count_hbm, count_ref, int_sem.at[0])
    owner_copy = pltpu.make_async_copy(owner_hbm, owner_ref, int_sem.at[1])
    count_copy.start()
    owner_copy.start()
    pl.semaphore_wait(barrier, len(peers))

    order = (2, 1, 3, 0)

    def x_copy(place, dc):
        to = (x + 4 - order[place]) % 4
        cc = (c + dc) % 2
        src = amp_ref.at[:, pl.ds(pl.multiple_of(to * WIDE + cc * HALF, LANES), HALF)]
        dst = raw.at[pl.ds(pl.multiple_of((place * 2 + c) * BLOCK, 16), BLOCK), :]
        if order[place] == 0 and dc == 0:
            return pltpu.make_async_copy(src, dst, xr.at[place * 2])
        return pltpu.make_async_remote_copy(
            src_ref=src, dst_ref=dst, send_sem=xs.at[place * 2 + dc], recv_sem=xr.at[place * 2 + dc],
            device_id=at(to, z, y, cc), device_id_type=MESH,
        )

    def x_wait(place, dc):
        dst = raw.at[pl.ds(pl.multiple_of((place * 2 + (c + dc) % 2) * BLOCK, 16), BLOCK), :]
        pltpu.make_async_copy(dst, dst, xr.at[place * 2 + dc]).wait()

    for dc in range(2):
        x_copy(0, dc).start()

    count_copy.wait()
    owner_copy.wait()

    row = lax.broadcasted_iota(I32, (LANES, LANES), 0)
    col = lax.broadcasted_iota(I32, (LANES, LANES), 1)
    holds = jnp.zeros((LANES, LANES), I32)
    for g in range(SECTORS):
        holds = jnp.where((row >> 4) == g, owner_ref[g], holds)
    perm[...] = jnp.where(((row & 15) == (col >> 3)) & (holds == (col & 7)), 1.0, 0.0).astype(BF16)

    sector = owner_ref[o // 4]
    live = count_ref[sector] * TILE
    live_row = live - x * WIDE
    live_col = live - (o % 4) * WIDE
    v_copy.wait()

    def mask(i, _):
        rows = pl.ds(pl.multiple_of(i * 64, 64), 64)
        r = lax.broadcasted_iota(I32, (64, WIDE), 0) + i * 64
        k = lax.broadcasted_iota(I32, (64, WIDE), 1)
        m = jnp.where((r < live_row) & (k < live_col), 1.0, 0.0).astype(BF16)
        v_ref[rows, :] = v_ref[rows, :] * m
        return 0

    lax.fori_loop(0, WIDE // 64, mask, 0)

    half = pl.ds(pl.multiple_of(c * HALF, LANES), HALF)
    half_other = pl.ds(pl.multiple_of((1 - c) * HALF, LANES), HALF)

    def slot(ch, zz, yy, cols):
        padded = PADDED[ch]
        return gots[ch].at[pl.ds(pl.multiple_of((zz * 4 + yy) * padded, 16), padded), cols]

    def zy_copy(ch, dz, rp):
        padded = PADDED[ch]
        to_z = (z + dz) % 4
        to_y = other if rp else y
        g = to_z * 2 + to_y // 2
        src = sends[ch].at[pl.ds(pl.multiple_of(g * padded, 16), padded), :]
        dst = slot(ch, z, (to_y % 2) * 2 + rp, half)
        i = ch * 8 + dz * 2 + rp
        if dz == 0 and rp == 0:
            return pltpu.make_async_copy(src, dst, zr.at[i])
        return pltpu.make_async_remote_copy(
            src_ref=src, dst_ref=dst, send_sem=zs.at[i], recv_sem=zr.at[i],
            device_id=at(x, to_z, to_y, c), device_id_type=MESH,
        )

    def landed(ch, dz, rp, mine, cols):
        return slot(ch, (z + 4 - dz) % 4, (yl if mine else 1 - yl) * 2 + rp, cols)

    def wait_for(ref, sem):
        pltpu.make_async_copy(ref, ref, sem).wait()

    def pass_on(ch, dz, rp, kind):
        i = ch * 8 + dz * 2 + rp
        ref = landed(ch, dz, rp, kind != "f", half)
        ss, rr, device = {
            "c": (cs, cr, at(x, z, y, 1 - c)),
            "y": (ys, yr, at(x, z, partner, c)),
            "f": (fs, fr, at(x, z, y, 1 - c)),
        }[kind]
        return pltpu.make_async_remote_copy(
            src_ref=ref, dst_ref=ref, send_sem=ss.at[i], recv_sem=rr.at[i],
            device_id=device, device_id_type=MESH,
        )

    def choose(ch):
        padded = PADDED[ch]
        for k in range(len(CHUNKS[ch])):
            for dc in range(2):
                x_wait(FIRST[ch] + k, dc)
        if ch == 0:
            for place in (1, 2, 3):
                for dc in range(2):
                    x_copy(place, dc).start()
        rows = len(CHUNKS[ch]) * 2 * BLOCK
        start = FIRST[ch] * 2 * BLOCK
        for b in range(padded // 16):
            depth = min(LANES, rows - b * LANES)
            picked = jnp.dot(
                perm[:, :depth], raw[start + b * LANES : start + b * LANES + depth, :],
                preferred_element_type=F32,
            ).astype(BF16)
            for g in range(SECTORS):
                sends[ch][g * padded + 16 * b : g * padded + 16 * b + 16, :] = picked[16 * g : 16 * g + 16, :]
        for dz, rp in PLACES:
            zy_copy(ch, dz, rp).start()

    def spread(ch, dz):
        for rp in range(2):
            wait_for(landed(ch, dz, rp, True, half), zr.at[ch * 8 + dz * 2 + rp])
            pass_on(ch, dz, rp, "y").start()
            pass_on(ch, dz, rp, "c").start()

    def forward(ch, dz):
        for rp in range(2):
            wait_for(landed(ch, dz, rp, False, half), yr.at[ch * 8 + dz * 2 + rp])
            pass_on(ch, dz, rp, "f").start()

    def collect(ch, dz):
        for rp in range(2):
            wait_for(landed(ch, dz, rp, True, half_other), cr.at[ch * 8 + dz * 2 + rp])
            wait_for(landed(ch, dz, rp, False, half_other), fr.at[ch * 8 + dz * 2 + rp])

    def multiply(ch, dz):
        height = 4 * PADDED[ch]
        rows = pl.ds(pl.multiple_of((z + 4 - dz) % 4 * height, 16), height)
        wide[:height, :] = jnp.dot(gots[ch][rows, :], v_ref[...], preferred_element_type=F32)

    def compact(ch, k):
        for side in range(2):

            @pl.when(yp == side)
            def _():
                for j in range(4):
                    to = Y_OF[side][j] * PAIR
                    start = j * PADDED[ch] + k * PAIR
                    prod[to : to + PAIR, :] = wide[start : start + PAIR, :]

    def encode(places, scale):
        tiles = WIDE // LANES // len(places)

        def biggest(i, m):
            rows = pl.ds(pl.multiple_of(i * 16, 16), 16)
            for j in range(WIDE // LANES):
                m = jnp.maximum(m, jnp.abs(prod[rows, j * LANES : (j + 1) * LANES]))
            return m

        top = lax.fori_loop(0, ZBLOCK // 16, biggest, jnp.full((16, LANES), 1e-30, F32))
        top = jnp.maximum(top[:8], top[8:])
        scale[...] = top * (1.0 / TOP)
        inv = TOP / top
        inv = jnp.concatenate([inv, inv], axis=0)

        def code(i, _):
            rows = pl.ds(pl.multiple_of(i * 16, 16), 16)
            for j in range(WIDE // LANES):
                value = jnp.round(prod[rows, j * LANES : (j + 1) * LANES] * inv)
                at_tile = (j % tiles) * LANES
                places[j // tiles][rows, at_tile : at_tile + LANES] = value.astype(I32).astype(I16)
            return 0

        lax.fori_loop(0, ZBLOCK // 16, code, 0)

    def add(codes, scale, first, tiles):
        step = scale[...]
        step = jnp.concatenate([step, step], axis=0)

        def body(i, _):
            rows = pl.ds(pl.multiple_of(i * 16, 16), 16)
            for j in range(tiles):
                value = codes[rows, j * LANES : (j + 1) * LANES].astype(I32).astype(F32) * step
                prod[rows, (first + j) * LANES : (first + j + 1) * LANES] += value
            return 0

        lax.fori_loop(0, ZBLOCK // 16, body, 0)

    def far_copies(k, i):
        to = (x + 1 + 2 * k) % 4
        j = i * 2 + k
        make = functools.partial(pltpu.make_async_remote_copy, device_id=at(to, z, y, c), device_id_type=MESH)
        return (
            make(src_ref=far_out.at[j], dst_ref=far_in.at[j], send_sem=fas.at[j], recv_sem=far_.at[j]),
            make(src_ref=far_out_s.at[i], dst_ref=far_in_s.at[j], send_sem=fass.at[j], recv_sem=fars.at[j]),
        )

    def near_copies(k, i):
        to = (x + 1 + 2 * k) % 4
        j = i * 2 + k
        make = functools.partial(pltpu.make_async_remote_copy, device_id=at(to, z, y, c), device_id_type=MESH)
        return (
            make(src_ref=near_out.at[j], dst_ref=near_in.at[j], send_sem=nes.at[j], recv_sem=ner.at[j]),
            make(src_ref=near_out_s.at[j], dst_ref=near_in_s.at[j], send_sem=ness.at[j], recv_sem=ners.at[j]),
        )

    def plane(i):
        return i + i // 2 - 2 * (i // 3)

    def far_step(i, _):
        dz = plane(i)

        @pl.when(i < 3)
        def _():
            spread(0, plane(i + 1))

        forward(0, dz)
        collect(0, dz)
        multiply(0, dz)
        compact(0, 0)
        encode((far_out.at[i * 2], far_out.at[i * 2 + 1]), far_out_s.at[i])
        for k in range(2):
            for copy in far_copies(k, i):
                copy.start()

        @pl.when(i == 1)
        def _():
            choose(1)

        @pl.when(i >= 2)
        def _():
            spread(1, plane(i - 2))

        return 0

    def near_step(i, _):
        dz = plane(i)

        @pl.when(i < 2)
        def _():
            spread(1, plane(i + 2))

        forward(1, dz)
        collect(1, dz)
        multiply(1, dz)
        for k in range(2):
            j = i * 2 + k
            compact(1, k)
            wait_for(far_in.at[j], far_.at[j])
            wait_for(far_in_s.at[j], fars.at[j])
            add(far_in.at[j], far_in_s.at[j], k * 7, 7)
            encode((near_out.at[j],), near_out_s.at[j])
            for copy in near_copies(k, i):
                copy.start()

        @pl.when(i == 0)
        def _():
            choose(2)

        @pl.when(i >= 1)
        def _():
            spread(2, plane(i - 1))

        return 0

    def out_copy(i):
        rows = pl.ds(pl.multiple_of((z + 4 - plane(i)) % 4 * ZBLOCK, 16), ZBLOCK)
        return pltpu.make_async_copy(done.at[i], out_ref.at[rows, :], out_sem.at[i])

    def last_step(i, _):
        dz = plane(i)

        @pl.when(i == 0)
        def _():
            spread(2, plane(3))

        forward(2, dz)
        collect(2, dz)
        multiply(2, dz)
        compact(2, 0)
        for k in range(2):
            j = i * 2 + k
            wait_for(near_in.at[j], ner.at[j])
            wait_for(near_in_s.at[j], ners.at[j])
            add(near_in.at[j], near_in_s.at[j], 0, WIDE // LANES)
        done[i] = prod[...].astype(BF16)
        out_copy(i).start()
        return 0

    choose(0)
    spread(0, 0)
    lax.fori_loop(0, 4, far_step, 0)
    lax.fori_loop(0, 4, near_step, 0)
    lax.fori_loop(0, 4, last_step, 0)

    for place in range(4):
        for dc in range(2):
            if order[place] or dc:
                x_copy(place, dc).wait_send()
    for ch in range(3):
        for dz, rp in PLACES:
            if dz or rp:
                zy_copy(ch, dz, rp).wait_send()
            for kind in "cyf":
                pass_on(ch, dz, rp, kind).wait_send()

    def sent(i, _):
        for k in range(2):
            for copy in far_copies(k, i):
                copy.wait_send()
            for copy in near_copies(k, i):
                copy.wait_send()
        out_copy(i).wait()
        return 0

    lax.fori_loop(0, 4, sent, 0)


Y_OF = ((0, 3, 1, 2), (2, 1, 3, 0))
PLACES = ((0, 0), (0, 1), (1, 0), (3, 0), (1, 1), (3, 1), (2, 0), (2, 1))


def per_device(amplitudes, integrals, nonzero_tile_count, sector_owner):
    dma = pltpu.SemaphoreType.DMA
    vmem = pltpu.VMEM
    codes = [vmem((8, ZBLOCK, cols), I16) for cols in (HALF, HALF, WIDE, WIDE)]
    scales = [vmem((n, 8, LANES), F32) for n in (4, 8, 8, 8)]
    out = pl.pallas_call(
        kernel,
        out_shape=jax.ShapeDtypeStruct((4 * ZBLOCK, WIDE), BF16),
        in_specs=[
            pl.BlockSpec(memory_space=pltpu.HBM),
            pl.BlockSpec(memory_space=pltpu.HBM),
            pl.BlockSpec(memory_space=pltpu.HBM),
            pl.BlockSpec(memory_space=pltpu.HBM),
        ],
        out_specs=pl.BlockSpec(memory_space=pl.ANY),
        scratch_shapes=[
            pltpu.SMEM((SECTORS,), I32),
            pltpu.SMEM((SECTORS,), I32),
            dma((2,)),
            vmem((8 * BLOCK, HALF), BF16),
            *[vmem((SECTORS * p, HALF), BF16) for p in PADDED],
            *[vmem((16 * p, WIDE), BF16) for p in PADDED],
            vmem((WIDE, WIDE), BF16),
            vmem((LANES, LANES), BF16),
            vmem((4 * max(PADDED), WIDE), F32),
            vmem((ZBLOCK, WIDE), F32),
            vmem((4, ZBLOCK, WIDE), BF16),
            dma((4,)),
            *codes,
            *scales,
            dma((1,)), dma((8,)), dma((8,)),
            *[dma((24,)) for _ in range(8)],
            *[dma((8,)) for _ in range(8)],
        ],
        compiler_params=pltpu.CompilerParams(
            collective_id=0, has_side_effects=True, vmem_limit_bytes=51 * 1024 * 1024
        ),
        cost_estimate=pl.CostEstimate(
            flops=2 * 16 * ZBLOCK * WIDE * WIDE, bytes_accessed=20_000_000, transcendentals=0
        ),
    )(
        pltpu.with_memory_space_constraint(nonzero_tile_count, pltpu.HBM),
        pltpu.with_memory_space_constraint(sector_owner, pltpu.HBM),
        amplitudes.reshape(BLOCK, amplitudes.shape[2]),
        integrals.reshape(WIDE, WIDE),
    )
    return out[:, None, :]


def solution(mesh):
    in_specs = (P(("vir", "occ"), None, None), P("occ", "vir", None), P(), P())
    out_specs = P("vir", "occ", None)
    return jax.shard_map(
        per_device, mesh=mesh, in_specs=in_specs, out_specs=out_specs, check_vma=False
    )
```

```python
import functools

import jax
import jax.numpy as jnp
from jax import lax
from jax.experimental import pallas as pl
from jax.experimental.pallas import tpu as pltpu
from jax.sharding import PartitionSpec as P

TILE = 64
MESH = pl.DeviceIdType.MESH
F32, BF16, I16, I32 = jnp.float32, jnp.bfloat16, jnp.int16, jnp.int32

ROWS = 18
SECTORS = 8
PAIR = 2 * ROWS
ZBLOCK = 4 * PAIR
HALF = 896
WIDE = 1792
LANES = 128
BLOCK = ROWS * SECTORS
TOP = 32752.0

CHUNKS = ((2,), (1, 3), (0,))
FIRST = (0, 1, 3)
PADDED = (48, 80, 48)


def kernel(
    count_hbm, owner_hbm, amp_ref, v_hbm, out_ref,
    count_ref, owner_ref, int_sem,
    raw, send0, send1, send2, got0, got1, got2, v_ref, perm, wide, prod, done, out_sem,
    far_out, far_in, near_out, near_in, far_out_s, far_in_s, near_out_s, near_in_s,
    v_sem, xs, xr, zs, cs, ys, fs, zr, yr, core_r, fas, far_, nes, ner, fass, fars, ness, ners,
):
    x = lax.axis_index("vir")
    o = lax.axis_index("occ")
    z, y, c = o // 8, (o // 2) % 4, o % 2
    yp, yl = y // 2, y % 2
    other = 3 - y
    partner = yp * 2 + 1 - yl
    sends = (send0, send1, send2)
    gots = (got0, got1, got2)

    def at(xx, zz, yy, cc):
        return (xx, (zz * 4 + yy) * 2 + cc)

    peers = [at((x + dx) % 4, z, y, (c + dc) % 2) for dx in range(4) for dc in range(2) if dx or dc]
    peers += [at(x, (z + dz) % 4, yy, c) for dz in range(4) for yy in (y, other) if dz or yy is other]
    peers += [at(x, z, partner, c)]
    barrier = pltpu.get_barrier_semaphore()
    for peer in peers:
        pl.semaphore_signal(barrier, inc=1, device_id=peer, device_id_type=MESH)

    v_copy = pltpu.make_async_copy(v_hbm, v_ref, v_sem.at[0])
    v_copy.start()
    count_copy = pltpu.make_async_copy(count_hbm, count_ref, int_sem.at[0])
    owner_copy = pltpu.make_async_copy(owner_hbm, owner_ref, int_sem.at[1])
    count_copy.start()
    owner_copy.start()
    pl.semaphore_wait(barrier, len(peers))

    order = (2, 1, 3, 0)

    def x_copy(place, dc):
        to = (x + 4 - order[place]) % 4
        cc = (c + dc) % 2
        src = amp_ref.at[:, pl.ds(pl.multiple_of(to * WIDE + cc * HALF, LANES), HALF)]
        dst = raw.at[pl.ds(pl.multiple_of((place * 2 + c) * BLOCK, 16), BLOCK), :]
        if order[place] == 0 and dc == 0:
            return pltpu.make_async_copy(src, dst, xr.at[place * 2])
        return pltpu.make_async_remote_copy(
            src_ref=src, dst_ref=dst, send_sem=xs.at[0], recv_sem=xr.at[place * 2 + dc],
            device_id=at(to, z, y, cc), device_id_type=MESH,
        )

    def x_wait(place, dc):
        dst = raw.at[pl.ds(pl.multiple_of((place * 2 + (c + dc) % 2) * BLOCK, 16), BLOCK), :]
        pltpu.make_async_copy(dst, dst, xr.at[place * 2 + dc]).wait()

    for dc in range(2):
        x_copy(0, dc).start()

    count_copy.wait()
    owner_copy.wait()

    row = lax.broadcasted_iota(I32, (LANES, LANES), 0)
    col = lax.broadcasted_iota(I32, (LANES, LANES), 1)
    holds = jnp.zeros((LANES, LANES), I32)
    for g in range(SECTORS):
        holds = jnp.where((row >> 4) == g, owner_ref[g], holds)
    perm[...] = jnp.where(((row & 15) == (col >> 3)) & (holds == (col & 7)), 1.0, 0.0).astype(BF16)

    sector = owner_ref[o // 4]
    live = count_ref[sector] * TILE
    live_row = live - x * WIDE
    live_col = live - (o % 4) * WIDE
    v_copy.wait()

    def mask(i, _):
        rows = pl.ds(pl.multiple_of(i * 64, 64), 64)
        r = lax.broadcasted_iota(I32, (64, WIDE), 0) + i * 64
        k = lax.broadcasted_iota(I32, (64, WIDE), 1)
        m = jnp.where((r < live_row) & (k < live_col), 1.0, 0.0).astype(BF16)
        v_ref[rows, :] = v_ref[rows, :] * m
        return 0

    lax.fori_loop(0, WIDE // 64, mask, 0)

    half = pl.ds(pl.multiple_of(c * HALF, LANES), HALF)
    half_other = pl.ds(pl.multiple_of((1 - c) * HALF, LANES), HALF)

    def slot(ch, zz, yy, cols):
        padded = PADDED[ch]
        return gots[ch].at[pl.ds(pl.multiple_of((zz * 4 + yy) * padded, 16), padded), cols]

    def zy_copy(ch, dz, rp):
        padded = PADDED[ch]
        to_z = (z + dz) % 4
        to_y = other if rp else y
        g = to_z * 2 + to_y // 2
        src = sends[ch].at[pl.ds(pl.multiple_of(g * padded, 16), padded), :]
        dst = slot(ch, z, (to_y % 2) * 2 + rp, half)
        i = ch * 8 + dz * 2 + rp
        if dz == 0 and rp == 0:
            return pltpu.make_async_copy(src, dst, zr.at[i])
        return pltpu.make_async_remote_copy(
            src_ref=src, dst_ref=dst, send_sem=zs.at[ch], recv_sem=zr.at[i],
            device_id=at(x, to_z, to_y, c), device_id_type=MESH,
        )

    def landed(ch, dz, rp, mine, cols):
        return slot(ch, (z + 4 - dz) % 4, (yl if mine else 1 - yl) * 2 + rp, cols)

    def wait_for(ref, sem):
        pltpu.make_async_copy(ref, ref, sem).wait()

    def pass_on(ch, dz, rp, kind):
        i = ch * 8 + dz * 2 + rp
        ref = landed(ch, dz, rp, kind != "f", half)
        ss, rr, device = {
            "c": (cs, core_r.at[ch * 4 + dz], at(x, z, y, 1 - c)),
            "y": (ys, yr.at[i], at(x, z, partner, c)),
            "f": (fs, core_r.at[ch * 4 + dz], at(x, z, y, 1 - c)),
        }[kind]
        return pltpu.make_async_remote_copy(
            src_ref=ref, dst_ref=ref, send_sem=ss.at[ch], recv_sem=rr,
            device_id=device, device_id_type=MESH,
        )

    def choose(ch):
        padded = PADDED[ch]
        for k in range(len(CHUNKS[ch])):
            for dc in range(2):
                x_wait(FIRST[ch] + k, dc)
        if ch == 0:
            for place in (1, 2, 3):
                for dc in range(2):
                    x_copy(place, dc).start()
        rows = len(CHUNKS[ch]) * 2 * BLOCK
        start = FIRST[ch] * 2 * BLOCK
        for b in range(padded // 16):
            depth = min(LANES, rows - b * LANES)
            picked = jnp.dot(
                perm[:, :depth], raw[start + b * LANES : start + b * LANES + depth, :],
                preferred_element_type=F32,
            ).astype(BF16)
            for g in range(SECTORS):
                sends[ch][g * padded + 16 * b : g * padded + 16 * b + 16, :] = picked[16 * g : 16 * g + 16, :]
        for dz, rp in PLACES:
            zy_copy(ch, dz, rp).start()

    def spread(ch, dz):
        for rp in range(2):
            wait_for(landed(ch, dz, rp, True, half), zr.at[ch * 8 + dz * 2 + rp])
            pass_on(ch, dz, rp, "y").start()
            pass_on(ch, dz, rp, "c").start()

    def forward(ch, dz):
        for rp in range(2):
            wait_for(landed(ch, dz, rp, False, half), yr.at[ch * 8 + dz * 2 + rp])
            pass_on(ch, dz, rp, "f").start()

    def collect(ch, dz):
        height = 4 * PADDED[ch]
        rows = pl.ds(pl.multiple_of((z + 4 - dz) % 4 * height, 16), height)
        wait_for(gots[ch].at[rows, half_other], core_r.at[ch * 4 + dz])

    def multiply(ch, dz):
        height = 4 * PADDED[ch]
        rows = pl.ds(pl.multiple_of((z + 4 - dz) % 4 * height, 16), height)
        wide[:height, :] = jnp.dot(gots[ch][rows, :], v_ref[...], preferred_element_type=F32)

    def compact(ch, k):
        for side in range(2):

            @pl.when(yp == side)
            def _():
                for j in range(4):
                    to = Y_OF[side][j] * PAIR
                    start = j * PADDED[ch] + k * PAIR
                    prod[to : to + PAIR, :] = wide[start : start + PAIR, :]

    def encode(places, scale):
        tiles = WIDE // LANES // len(places)

        def biggest(i, m):
            rows = pl.ds(pl.multiple_of(i * 16, 16), 16)
            for j in range(WIDE // LANES):
                m = jnp.maximum(m, jnp.abs(prod[rows, j * LANES : (j + 1) * LANES]))
            return m

        top = lax.fori_loop(0, ZBLOCK // 16, biggest, jnp.full((16, LANES), 1e-30, F32))
        top = jnp.maximum(top[:8], top[8:])
        scale[...] = top * (1.0 / TOP)
        inv = TOP / top
        inv = jnp.concatenate([inv, inv], axis=0)

        def code(i, _):
            rows = pl.ds(pl.multiple_of(i * 16, 16), 16)
            for j in range(WIDE // LANES):
                value = jnp.round(prod[rows, j * LANES : (j + 1) * LANES] * inv)
                at_tile = (j % tiles) * LANES
                places[j // tiles][rows, at_tile : at_tile + LANES] = value.astype(I32).astype(I16)
            return 0

        lax.fori_loop(0, ZBLOCK // 16, code, 0)

    def add(codes, scale, first, tiles):
        step = scale[...]
        step = jnp.concatenate([step, step], axis=0)

        def body(i, _):
            rows = pl.ds(pl.multiple_of(i * 16, 16), 16)
            for j in range(tiles):
                value = codes[rows, j * LANES : (j + 1) * LANES].astype(I32).astype(F32) * step
                prod[rows, (first + j) * LANES : (first + j + 1) * LANES] += value
            return 0

        lax.fori_loop(0, ZBLOCK // 16, body, 0)

    def far_copies(k, i):
        to = (x + 1 + 2 * k) % 4
        j = i * 2 + k
        make = functools.partial(pltpu.make_async_remote_copy, device_id=at(to, z, y, c), device_id_type=MESH)
        return (
            make(src_ref=far_out.at[j], dst_ref=far_in.at[j], send_sem=fas.at[0], recv_sem=far_.at[j]),
            make(src_ref=far_out_s.at[i], dst_ref=far_in_s.at[j], send_sem=fass.at[0], recv_sem=fars.at[j]),
        )

    def near_copies(k, i):
        to = (x + 1 + 2 * k) % 4
        j = i * 2 + k
        make = functools.partial(pltpu.make_async_remote_copy, device_id=at(to, z, y, c), device_id_type=MESH)
        return (
            make(src_ref=near_out.at[j], dst_ref=near_in.at[j], send_sem=nes.at[0], recv_sem=ner.at[j]),
            make(src_ref=near_out_s.at[j], dst_ref=near_in_s.at[j], send_sem=ness.at[0], recv_sem=ners.at[j]),
        )

    def plane(i):
        return i + i // 2 - 2 * (i // 3)

    def far_step(i, _):
        dz = plane(i)

        @pl.when(i < 3)
        def _():
            spread(0, plane(i + 1))

        forward(0, dz)
        collect(0, dz)
        multiply(0, dz)
        compact(0, 0)
        encode((far_out.at[i * 2], far_out.at[i * 2 + 1]), far_out_s.at[i])
        for k in range(2):
            for copy in far_copies(k, i):
                copy.start()

        @pl.when(i == 1)
        def _():
            choose(1)

        @pl.when(i >= 2)
        def _():
            spread(1, plane(i - 2))

        return 0

    def near_step(i, _):
        dz = plane(i)

        @pl.when(i < 2)
        def _():
            spread(1, plane(i + 2))

        forward(1, dz)
        collect(1, dz)
        multiply(1, dz)
        for k in range(2):
            j = i * 2 + k
            compact(1, k)
            wait_for(far_in.at[j], far_.at[j])
            wait_for(far_in_s.at[j], fars.at[j])
            add(far_in.at[j], far_in_s.at[j], k * 7, 7)
            encode((near_out.at[j],), near_out_s.at[j])
            for copy in near_copies(k, i):
                copy.start()

        @pl.when(i == 0)
        def _():
            choose(2)

        @pl.when(i >= 1)
        def _():
            spread(2, plane(i - 1))

        return 0

    def out_copy(i):
        rows = pl.ds(pl.multiple_of((z + 4 - plane(i)) % 4 * ZBLOCK, 16), ZBLOCK)
        return pltpu.make_async_copy(done.at[i], out_ref.at[rows, :], out_sem.at[0])

    def last_step(i, _):
        dz = plane(i)

        @pl.when(i == 0)
        def _():
            spread(2, plane(3))

        forward(2, dz)
        collect(2, dz)
        multiply(2, dz)
        compact(2, 0)
        for k in range(2):
            j = i * 2 + k
            wait_for(near_in.at[j], ner.at[j])
            wait_for(near_in_s.at[j], ners.at[j])
            add(near_in.at[j], near_in_s.at[j], 0, WIDE // LANES)
        done[i] = prod[...].astype(BF16)
        out_copy(i).start()
        return 0

    choose(0)
    spread(0, 0)
    lax.fori_loop(0, 4, far_step, 0)
    lax.fori_loop(0, 4, near_step, 0)
    lax.fori_loop(0, 4, last_step, 0)

    wait_for(raw.at[: 7 * BLOCK, :], xs.at[0])
    for ch in range(3):
        wait_for(sends[ch].at[: 7 * PADDED[ch], :], zs.at[ch])
        for sem in (cs, ys, fs):
            wait_for(sends[ch], sem.at[ch])
    wait_for(far_out, fas.at[0])
    wait_for(near_out, nes.at[0])
    wait_for(near_out_s, fass.at[0])
    wait_for(near_out_s, ness.at[0])
    wait_for(done, out_sem.at[0])


Y_OF = ((0, 3, 1, 2), (2, 1, 3, 0))
PLACES = ((0, 0), (0, 1), (1, 0), (3, 0), (1, 1), (3, 1), (2, 0), (2, 1))


def per_device(amplitudes, integrals, nonzero_tile_count, sector_owner):
    dma = pltpu.SemaphoreType.DMA
    vmem = pltpu.VMEM
    codes = [vmem((8, ZBLOCK, cols), I16) for cols in (HALF, HALF, WIDE, WIDE)]
    scales = [vmem((n, 8, LANES), F32) for n in (4, 8, 8, 8)]
    out = pl.pallas_call(
        kernel,
        out_shape=jax.ShapeDtypeStruct((4 * ZBLOCK, WIDE), BF16),
        in_specs=[
            pl.BlockSpec(memory_space=pltpu.HBM),
            pl.BlockSpec(memory_space=pltpu.HBM),
            pl.BlockSpec(memory_space=pltpu.HBM),
            pl.BlockSpec(memory_space=pltpu.HBM),
        ],
        out_specs=pl.BlockSpec(memory_space=pl.ANY),
        scratch_shapes=[
            pltpu.SMEM((SECTORS,), I32),
            pltpu.SMEM((SECTORS,), I32),
            dma((2,)),
            vmem((8 * BLOCK, HALF), BF16),
            *[vmem((SECTORS * p, HALF), BF16) for p in PADDED],
            *[vmem((16 * p, WIDE), BF16) for p in PADDED],
            vmem((WIDE, WIDE), BF16),
            vmem((LANES, LANES), BF16),
            vmem((4 * max(PADDED), WIDE), F32),
            vmem((ZBLOCK, WIDE), F32),
            vmem((4, ZBLOCK, WIDE), BF16),
            dma((1,)),
            *codes,
            *scales,
            *[dma((n,)) for n in (1, 1, 8, 3, 3, 3, 3, 24, 24, 12)],
            *[dma((n,)) for n in (1, 8) * 4],
        ],
        compiler_params=pltpu.CompilerParams(
            collective_id=0, has_side_effects=True, vmem_limit_bytes=51 * 1024 * 1024
        ),
        cost_estimate=pl.CostEstimate(
            flops=2 * 16 * ZBLOCK * WIDE * WIDE, bytes_accessed=20_000_000, transcendentals=0
        ),
    )(
        pltpu.with_memory_space_constraint(nonzero_tile_count, pltpu.HBM),
        pltpu.with_memory_space_constraint(sector_owner, pltpu.HBM),
        amplitudes.reshape(BLOCK, amplitudes.shape[2]),
        integrals.reshape(WIDE, WIDE),
    )
    return out[:, None, :]


def solution(mesh):
    in_specs = (P(("vir", "occ"), None, None), P("occ", "vir", None), P(), P())
    out_specs = P("vir", "occ", None)
    return jax.shard_map(
        per_device, mesh=mesh, in_specs=in_specs, out_specs=out_specs, check_vma=False
    )
```

```python
import functools

import jax
import jax.numpy as jnp
from jax import lax
from jax.experimental import pallas as pl
from jax.experimental.pallas import tpu as pltpu
from jax.sharding import PartitionSpec as P

TILE = 64
MESH = pl.DeviceIdType.MESH
F32, BF16, I16, I32 = jnp.float32, jnp.bfloat16, jnp.int16, jnp.int32

ROWS = 18
SECTORS = 8
PAIR = 2 * ROWS
ZBLOCK = 4 * PAIR
HALF = 896
WIDE = 1792
LANES = 128
BLOCK = ROWS * SECTORS
TOP = 32752.0

CHUNKS = ((2,), (1, 3), (0,))
FIRST = (0, 1, 3)
PADDED = (48, 80, 48)


def kernel(
    count_hbm, owner_hbm, amp_ref, v_hbm, out_ref,
    count_ref, owner_ref, int_sem,
    raw, send0, send1, send2, got0, got1, got2, v_ref, perm, wide, prod, done, out_sem,
    far_out, far_in, near_out, near_in, far_out_s, far_in_s, near_out_s, near_in_s,
    v_sem, xs, xr, zs, cs, ys, fs, zr, yr, core_r, fas, far_, nes, ner, fass, fars, ness, ners,
):
    x = lax.axis_index("vir")
    o = lax.axis_index("occ")
    z, y, c = o // 8, (o // 2) % 4, o % 2
    yp, yl = y // 2, y % 2
    other = 3 - y
    partner = yp * 2 + 1 - yl
    sends = (send0, send1, send2)
    gots = (got0, got1, got2)

    def at(xx, zz, yy, cc):
        return (xx, (zz * 4 + yy) * 2 + cc)

    peers = [at((x + dx) % 4, z, y, (c + dc) % 2) for dx in range(4) for dc in range(2) if dx or dc]
    peers += [at(x, (z + dz) % 4, yy, c) for dz in range(4) for yy in (y, other) if dz or yy is other]
    peers += [at(x, z, partner, c)]
    barrier = pltpu.get_barrier_semaphore()
    for peer in peers:
        pl.semaphore_signal(barrier, inc=1, device_id=peer, device_id_type=MESH)

    v_copy = pltpu.make_async_copy(v_hbm, v_ref, v_sem.at[0])
    v_copy.start()
    count_copy = pltpu.make_async_copy(count_hbm, count_ref, int_sem.at[0])
    owner_copy = pltpu.make_async_copy(owner_hbm, owner_ref, int_sem.at[1])
    count_copy.start()
    owner_copy.start()
    pl.semaphore_wait(barrier, len(peers))

    order = (2, 1, 3, 0)

    def x_copy(place, dc):
        to = (x + 4 - order[place]) % 4
        cc = (c + dc) % 2
        src = amp_ref.at[:, pl.ds(pl.multiple_of(to * WIDE + cc * HALF, LANES), HALF)]
        dst = raw.at[pl.ds(pl.multiple_of((place * 2 + c) * BLOCK, 16), BLOCK), :]
        if order[place] == 0 and dc == 0:
            return pltpu.make_async_copy(src, dst, xr.at[place * 2])
        return pltpu.make_async_remote_copy(
            src_ref=src, dst_ref=dst, send_sem=xs.at[0], recv_sem=xr.at[place * 2 + dc],
            device_id=at(to, z, y, cc), device_id_type=MESH,
        )

    def x_wait(place, dc):
        dst = raw.at[pl.ds(pl.multiple_of((place * 2 + (c + dc) % 2) * BLOCK, 16), BLOCK), :]
        pltpu.make_async_copy(dst, dst, xr.at[place * 2 + dc]).wait()

    for dc in range(2):
        x_copy(0, dc).start()

    count_copy.wait()
    owner_copy.wait()

    row = lax.broadcasted_iota(I32, (LANES, LANES), 0)
    col = lax.broadcasted_iota(I32, (LANES, LANES), 1)
    holds = jnp.zeros((LANES, LANES), I32)
    for g in range(SECTORS):
        holds = jnp.where((row >> 4) == g, owner_ref[g], holds)
    perm[...] = jnp.where(((row & 15) == (col >> 3)) & (holds == (col & 7)), 1.0, 0.0).astype(BF16)

    sector = owner_ref[o // 4]
    live = count_ref[sector] * TILE
    live_row = live - x * WIDE
    live_col = live - (o % 4) * WIDE
    v_copy.wait()

    def mask(i, _):
        rows = pl.ds(pl.multiple_of(i * 64, 64), 64)
        r = lax.broadcasted_iota(I32, (64, WIDE), 0) + i * 64
        k = lax.broadcasted_iota(I32, (64, WIDE), 1)
        m = jnp.where((r < live_row) & (k < live_col), 1.0, 0.0).astype(BF16)
        v_ref[rows, :] = v_ref[rows, :] * m
        return 0

    lax.fori_loop(0, WIDE // 64, mask, 0)

    half = pl.ds(pl.multiple_of(c * HALF, LANES), HALF)
    half_other = pl.ds(pl.multiple_of((1 - c) * HALF, LANES), HALF)

    def slot(ch, zz, yy, cols):
        padded = PADDED[ch]
        return gots[ch].at[pl.ds(pl.multiple_of((zz * 4 + yy) * padded, 16), padded), cols]

    def zy_copy(ch, dz, rp):
        padded = PADDED[ch]
        to_z = (z + dz) % 4
        to_y = other if rp else y
        g = to_z * 2 + to_y // 2
        src = sends[ch].at[pl.ds(pl.multiple_of(g * padded, 16), padded), :]
        dst = slot(ch, z, (to_y % 2) * 2 + rp, half)
        i = ch * 8 + dz * 2 + rp
        if dz == 0 and rp == 0:
            return pltpu.make_async_copy(src, dst, zr.at[i])
        return pltpu.make_async_remote_copy(
            src_ref=src, dst_ref=dst, send_sem=zs.at[ch], recv_sem=zr.at[i],
            device_id=at(x, to_z, to_y, c), device_id_type=MESH,
        )

    def landed(ch, dz, rp, mine, cols):
        return slot(ch, (z + 4 - dz) % 4, (yl if mine else 1 - yl) * 2 + rp, cols)

    def wait_for(ref, sem):
        pltpu.make_async_copy(ref, ref, sem).wait()

    def pass_on(ch, dz, rp, kind):
        i = ch * 8 + dz * 2 + rp
        ref = landed(ch, dz, rp, kind != "f", half)
        ss, rr, device = {
            "c": (cs, core_r.at[ch * 4 + dz], at(x, z, y, 1 - c)),
            "y": (ys, yr.at[i], at(x, z, partner, c)),
            "f": (fs, core_r.at[ch * 4 + dz], at(x, z, y, 1 - c)),
        }[kind]
        return pltpu.make_async_remote_copy(
            src_ref=ref, dst_ref=ref, send_sem=ss.at[ch], recv_sem=rr,
            device_id=device, device_id_type=MESH,
        )

    def choose(ch):
        padded = PADDED[ch]
        for k in range(len(CHUNKS[ch])):
            for dc in range(2):
                x_wait(FIRST[ch] + k, dc)
        if ch == 0:
            for place in (1, 2, 3):
                for dc in range(2):
                    x_copy(place, dc).start()
        rows = len(CHUNKS[ch]) * 2 * BLOCK
        start = FIRST[ch] * 2 * BLOCK
        for b in range(padded // 16):
            depth = min(LANES, rows - b * LANES)
            picked = jnp.dot(
                perm[:, :depth], raw[start + b * LANES : start + b * LANES + depth, :],
                preferred_element_type=F32,
            ).astype(BF16)
            for g in range(SECTORS):
                sends[ch][g * padded + 16 * b : g * padded + 16 * b + 16, :] = picked[16 * g : 16 * g + 16, :]
        for dz, rp in PLACES:
            zy_copy(ch, dz, rp).start()

    def spread(ch, dz):
        for rp in range(2):
            wait_for(landed(ch, dz, rp, True, half), zr.at[ch * 8 + dz * 2 + rp])
            pass_on(ch, dz, rp, "y").start()
            pass_on(ch, dz, rp, "c").start()

    def forward(ch, dz):
        for rp in range(2):
            wait_for(landed(ch, dz, rp, False, half), yr.at[ch * 8 + dz * 2 + rp])
            pass_on(ch, dz, rp, "f").start()

    def collect(ch, dz):
        height = 4 * PADDED[ch]
        rows = pl.ds(pl.multiple_of((z + 4 - dz) % 4 * height, 16), height)
        wait_for(gots[ch].at[rows, half_other], core_r.at[ch * 4 + dz])

    def multiply(ch, dz):
        height = 4 * PADDED[ch]
        rows = pl.ds(pl.multiple_of((z + 4 - dz) % 4 * height, 16), height)
        wide[:height, :] = jnp.dot(gots[ch][rows, :], v_ref[...], preferred_element_type=F32)

    def compact(ch, k):
        for side in range(2):

            @pl.when(yp == side)
            def _():
                for j in range(4):
                    to = Y_OF[side][j] * PAIR
                    start = j * PADDED[ch] + k * PAIR
                    prod[to : to + PAIR, :] = wide[start : start + PAIR, :]

    def encode(places, scale):
        tiles = WIDE // LANES // len(places)

        def biggest(i, m):
            rows = pl.ds(pl.multiple_of(i * 16, 16), 16)
            for j in range(WIDE // LANES):
                m = jnp.maximum(m, jnp.abs(prod[rows, j * LANES : (j + 1) * LANES]))
            return m

        top = lax.fori_loop(0, ZBLOCK // 16, biggest, jnp.full((16, LANES), 1e-30, F32))
        top = jnp.max(top, axis=0, keepdims=True)
        scale[...] = top * (1.0 / TOP)
        inv = TOP / top
        inv = jnp.broadcast_to(inv, (16, LANES))

        def code(i, _):
            rows = pl.ds(pl.multiple_of(i * 16, 16), 16)
            for j in range(WIDE // LANES):
                value = jnp.round(prod[rows, j * LANES : (j + 1) * LANES] * inv)
                at_tile = (j % tiles) * LANES
                places[j // tiles][rows, at_tile : at_tile + LANES] = value.astype(I32).astype(I16)
            return 0

        lax.fori_loop(0, ZBLOCK // 16, code, 0)

    def add(codes, scale, first, tiles):
        step = jnp.broadcast_to(scale[...], (16, LANES))

        def body(i, _):
            rows = pl.ds(pl.multiple_of(i * 16, 16), 16)
            for j in range(tiles):
                value = codes[rows, j * LANES : (j + 1) * LANES].astype(I32).astype(F32) * step
                prod[rows, (first + j) * LANES : (first + j + 1) * LANES] += value
            return 0

        lax.fori_loop(0, ZBLOCK // 16, body, 0)

    def far_copies(k, i):
        to = (x + 1 + 2 * k) % 4
        j = i * 2 + k
        make = functools.partial(pltpu.make_async_remote_copy, device_id=at(to, z, y, c), device_id_type=MESH)
        return (
            make(src_ref=far_out.at[j], dst_ref=far_in.at[j], send_sem=fas.at[0], recv_sem=far_.at[j]),
            make(src_ref=far_out_s.at[i], dst_ref=far_in_s.at[j], send_sem=fass.at[0], recv_sem=fars.at[j]),
        )

    def near_copies(k, i):
        to = (x + 1 + 2 * k) % 4
        j = i * 2 + k
        make = functools.partial(pltpu.make_async_remote_copy, device_id=at(to, z, y, c), device_id_type=MESH)
        return (
            make(src_ref=near_out.at[j], dst_ref=near_in.at[j], send_sem=nes.at[0], recv_sem=ner.at[j]),
            make(src_ref=near_out_s.at[j], dst_ref=near_in_s.at[j], send_sem=ness.at[0], recv_sem=ners.at[j]),
        )

    def plane(i):
        return i + i // 2 - 2 * (i // 3)

    def far_step(i, _):
        dz = plane(i)

        @pl.when(i < 3)
        def _():
            spread(0, plane(i + 1))

        forward(0, dz)
        collect(0, dz)
        multiply(0, dz)
        compact(0, 0)
        encode((far_out.at[i * 2], far_out.at[i * 2 + 1]), far_out_s.at[i])
        for k in range(2):
            for copy in far_copies(k, i):
                copy.start()

        @pl.when(i == 1)
        def _():
            choose(1)

        @pl.when(i >= 2)
        def _():
            spread(1, plane(i - 2))

        return 0

    def near_step(i, _):
        dz = plane(i)

        @pl.when(i < 2)
        def _():
            spread(1, plane(i + 2))

        forward(1, dz)
        collect(1, dz)
        multiply(1, dz)
        for k in range(2):
            j = i * 2 + k
            compact(1, k)
            wait_for(far_in.at[j], far_.at[j])
            wait_for(far_in_s.at[j], fars.at[j])
            add(far_in.at[j], far_in_s.at[j], k * 7, 7)
            encode((near_out.at[j],), near_out_s.at[j])
            for copy in near_copies(k, i):
                copy.start()

        @pl.when(i == 0)
        def _():
            choose(2)

        @pl.when(i >= 1)
        def _():
            spread(2, plane(i - 1))

        return 0

    def out_copy(i):
        rows = pl.ds(pl.multiple_of((z + 4 - plane(i)) % 4 * ZBLOCK, 16), ZBLOCK)
        return pltpu.make_async_copy(done.at[i], out_ref.at[rows, :], out_sem.at[0])

    def finish(i):
        left, right = i * 2, i * 2 + 1
        steps = [jnp.broadcast_to(near_in_s[j], (16, LANES)) for j in (left, right)]

        def body(n, _):
            rows = pl.ds(pl.multiple_of(n * 16, 16), 16)
            for j in range(WIDE // LANES):
                cols = slice(j * LANES, (j + 1) * LANES)
                total = prod[rows, cols]
                for m, step in zip((left, right), steps):
                    total += near_in[m, rows, cols].astype(I32).astype(F32) * step
                done[i, rows, cols] = total.astype(BF16)
            return 0

        lax.fori_loop(0, ZBLOCK // 16, body, 0)

    def last_step(i, _):
        dz = plane(i)

        @pl.when(i == 0)
        def _():
            spread(2, plane(3))

        forward(2, dz)
        collect(2, dz)
        multiply(2, dz)
        compact(2, 0)
        for k in range(2):
            j = i * 2 + k
            wait_for(near_in.at[j], ner.at[j])
            wait_for(near_in_s.at[j], ners.at[j])
        finish(i)
        out_copy(i).start()
        return 0

    choose(0)
    spread(0, 0)
    lax.fori_loop(0, 4, far_step, 0)
    lax.fori_loop(0, 4, near_step, 0)
    lax.fori_loop(0, 4, last_step, 0)

    wait_for(raw.at[: 7 * BLOCK, :], xs.at[0])
    for ch in range(3):
        wait_for(sends[ch].at[: 7 * PADDED[ch], :], zs.at[ch])
        for sem in (cs, ys, fs):
            wait_for(sends[ch], sem.at[ch])
    wait_for(far_out, fas.at[0])
    wait_for(near_out, nes.at[0])
    wait_for(near_out_s, fass.at[0])
    wait_for(near_out_s, ness.at[0])
    wait_for(done, out_sem.at[0])


Y_OF = ((0, 3, 1, 2), (2, 1, 3, 0))
PLACES = ((0, 0), (0, 1), (1, 0), (3, 0), (1, 1), (3, 1), (2, 0), (2, 1))


def per_device(amplitudes, integrals, nonzero_tile_count, sector_owner):
    dma = pltpu.SemaphoreType.DMA
    vmem = pltpu.VMEM
    codes = [vmem((8, ZBLOCK, cols), I16) for cols in (HALF, HALF, WIDE, WIDE)]
    scales = [vmem((n, 1, LANES), F32) for n in (4, 8, 8, 8)]
    out = pl.pallas_call(
        kernel,
        out_shape=jax.ShapeDtypeStruct((4 * ZBLOCK, WIDE), BF16),
        in_specs=[
            pl.BlockSpec(memory_space=pltpu.HBM),
            pl.BlockSpec(memory_space=pltpu.HBM),
            pl.BlockSpec(memory_space=pltpu.HBM),
            pl.BlockSpec(memory_space=pltpu.HBM),
        ],
        out_specs=pl.BlockSpec(memory_space=pl.ANY),
        scratch_shapes=[
            pltpu.SMEM((SECTORS,), I32),
            pltpu.SMEM((SECTORS,), I32),
            dma((2,)),
            vmem((8 * BLOCK, HALF), BF16),
            *[vmem((SECTORS * p, HALF), BF16) for p in PADDED],
            *[vmem((16 * p, WIDE), BF16) for p in PADDED],
            vmem((WIDE, WIDE), BF16),
            vmem((LANES, LANES), BF16),
            vmem((4 * max(PADDED), WIDE), F32),
            vmem((ZBLOCK, WIDE), F32),
            vmem((4, ZBLOCK, WIDE), BF16),
            dma((1,)),
            *codes,
            *scales,
            *[dma((n,)) for n in (1, 1, 8, 3, 3, 3, 3, 24, 24, 12)],
            *[dma((n,)) for n in (1, 8) * 4],
        ],
        compiler_params=pltpu.CompilerParams(
            collective_id=0, has_side_effects=True, vmem_limit_bytes=51 * 1024 * 1024
        ),
        cost_estimate=pl.CostEstimate(
            flops=2 * 16 * ZBLOCK * WIDE * WIDE, bytes_accessed=20_000_000, transcendentals=0
        ),
    )(
        pltpu.with_memory_space_constraint(nonzero_tile_count, pltpu.HBM),
        pltpu.with_memory_space_constraint(sector_owner, pltpu.HBM),
        amplitudes.reshape(BLOCK, amplitudes.shape[2]),
        integrals.reshape(WIDE, WIDE),
    )
    return out[:, None, :]


def solution(mesh):
    in_specs = (P(("vir", "occ"), None, None), P("occ", "vir", None), P(), P())
    out_specs = P("vir", "occ", None)
    return jax.shard_map(
        per_device, mesh=mesh, in_specs=in_specs, out_specs=out_specs, check_vma=False
    )
```

```python
import functools

import jax
import jax.numpy as jnp
from jax import lax
from jax.experimental import pallas as pl
from jax.experimental.pallas import tpu as pltpu
from jax.sharding import PartitionSpec as P

TILE = 64
MESH = pl.DeviceIdType.MESH
F32, BF16, I16, I32 = jnp.float32, jnp.bfloat16, jnp.int16, jnp.int32

ROWS = 18
SECTORS = 8
PAIR = 2 * ROWS
ZBLOCK = 4 * PAIR
HALF = 896
WIDE = 1792
LANES = 128
BLOCK = ROWS * SECTORS
TOP = 32752.0

CHUNKS = ((2,), (1, 3), (0,))
FIRST = (0, 1, 3)
PADDED = (48, 80, 48)


def kernel(
    count_hbm, owner_hbm, amp_ref, v_hbm, out_ref,
    count_ref, owner_ref, int_sem,
    raw, send0, send1, send2, got0, got1, got2, v_ref, perm, wide, prod, done, out_sem,
    far_out, far_in, near_out, near_in, far_out_s, far_in_s, near_out_s, near_in_s,
    v_sem, xs, xr, zs, cs, ys, fs, zr, yr, core_r, fas, far_, nes, ner, fass, fars, ness, ners,
):
    x = lax.axis_index("vir")
    o = lax.axis_index("occ")
    z, y, c = o // 8, (o // 2) % 4, o % 2
    yp, yl = y // 2, y % 2
    other = 3 - y
    partner = yp * 2 + 1 - yl
    sends = (send0, send1, send2)
    gots = (got0, got1, got2)

    def at(xx, zz, yy, cc):
        return (xx, (zz * 4 + yy) * 2 + cc)

    peers = [at((x + dx) % 4, z, y, (c + dc) % 2) for dx in range(4) for dc in range(2) if dx or dc]
    peers += [at(x, (z + dz) % 4, yy, c) for dz in range(4) for yy in (y, other) if dz or yy is other]
    peers += [at(x, z, partner, c)]
    barrier = pltpu.get_barrier_semaphore()
    for peer in peers:
        pl.semaphore_signal(barrier, inc=1, device_id=peer, device_id_type=MESH)

    v_copy = pltpu.make_async_copy(v_hbm, v_ref, v_sem.at[0])
    v_copy.start()
    count_copy = pltpu.make_async_copy(count_hbm, count_ref, int_sem.at[0])
    owner_copy = pltpu.make_async_copy(owner_hbm, owner_ref, int_sem.at[1])
    count_copy.start()
    owner_copy.start()
    pl.semaphore_wait(barrier, len(peers))

    order = (2, 1, 3, 0)

    def x_copy(place, dc):
        to = (x + 4 - order[place]) % 4
        cc = (c + dc) % 2
        src = amp_ref.at[:, pl.ds(pl.multiple_of(to * WIDE + cc * HALF, LANES), HALF)]
        dst = raw.at[pl.ds(pl.multiple_of((place * 2 + c) * BLOCK, 16), BLOCK), :]
        if order[place] == 0 and dc == 0:
            return pltpu.make_async_copy(src, dst, xr.at[place * 2])
        return pltpu.make_async_remote_copy(
            src_ref=src, dst_ref=dst, send_sem=xs.at[0], recv_sem=xr.at[place * 2 + dc],
            device_id=at(to, z, y, cc), device_id_type=MESH,
        )

    def x_wait(place, dc):
        dst = raw.at[pl.ds(pl.multiple_of((place * 2 + (c + dc) % 2) * BLOCK, 16), BLOCK), :]
        pltpu.make_async_copy(dst, dst, xr.at[place * 2 + dc]).wait()

    for dc in range(2):
        x_copy(0, dc).start()

    count_copy.wait()
    owner_copy.wait()

    row = lax.broadcasted_iota(I32, (LANES, LANES), 0)
    col = lax.broadcasted_iota(I32, (LANES, LANES), 1)
    holds = jnp.zeros((LANES, LANES), I32)
    for g in range(SECTORS):
        holds = jnp.where((row >> 4) == g, owner_ref[g], holds)
    perm[...] = jnp.where(((row & 15) == (col >> 3)) & (holds == (col & 7)), 1.0, 0.0).astype(BF16)

    sector = owner_ref[o // 4]
    live = count_ref[sector] * TILE
    live_row = live - x * WIDE
    live_col = live - (o % 4) * WIDE
    v_copy.wait()

    def mask(i, _):
        rows = pl.ds(pl.multiple_of(i * 64, 64), 64)
        r = lax.broadcasted_iota(I32, (64, WIDE), 0) + i * 64
        k = lax.broadcasted_iota(I32, (64, WIDE), 1)
        m = jnp.where((r < live_row) & (k < live_col), 1.0, 0.0).astype(BF16)
        v_ref[rows, :] = v_ref[rows, :] * m
        return 0

    lax.fori_loop(0, WIDE // 64, mask, 0)

    half = pl.ds(pl.multiple_of(c * HALF, LANES), HALF)
    half_other = pl.ds(pl.multiple_of((1 - c) * HALF, LANES), HALF)

    def slot(ch, zz, yy, cols):
        padded = PADDED[ch]
        return gots[ch].at[pl.ds(pl.multiple_of((zz * 4 + yy) * padded, 16), padded), cols]

    def zy_copy(ch, dz, rp):
        padded = PADDED[ch]
        to_z = (z + dz) % 4
        to_y = other if rp else y
        g = to_z * 2 + to_y // 2
        src = sends[ch].at[pl.ds(pl.multiple_of(g * padded, 16), padded), :]
        dst = slot(ch, z, (to_y % 2) * 2 + rp, half)
        i = ch * 8 + dz * 2 + rp
        if dz == 0 and rp == 0:
            return pltpu.make_async_copy(src, dst, zr.at[i])
        return pltpu.make_async_remote_copy(
            src_ref=src, dst_ref=dst, send_sem=zs.at[ch], recv_sem=zr.at[i],
            device_id=at(x, to_z, to_y, c), device_id_type=MESH,
        )

    def landed(ch, dz, rp, mine, cols):
        return slot(ch, (z + 4 - dz) % 4, (yl if mine else 1 - yl) * 2 + rp, cols)

    def wait_for(ref, sem):
        pltpu.make_async_copy(ref, ref, sem).wait()

    def pass_on(ch, dz, rp, kind):
        i = ch * 8 + dz * 2 + rp
        ref = landed(ch, dz, rp, kind != "f", half)
        ss, rr, device = {
            "c": (cs, core_r.at[ch * 4 + dz], at(x, z, y, 1 - c)),
            "y": (ys, yr.at[i], at(x, z, partner, c)),
            "f": (fs, core_r.at[ch * 4 + dz], at(x, z, y, 1 - c)),
        }[kind]
        return pltpu.make_async_remote_copy(
            src_ref=ref, dst_ref=ref, send_sem=ss.at[ch], recv_sem=rr,
            device_id=device, device_id_type=MESH,
        )

    def spread_one(ch, dz, rp):
        wait_for(landed(ch, dz, rp, True, half), zr.at[ch * 8 + dz * 2 + rp])
        pass_on(ch, dz, rp, "y").start()
        pass_on(ch, dz, rp, "c").start()

    def choose(ch):
        padded = PADDED[ch]
        for k in range(len(CHUNKS[ch])):
            for dc in range(2):
                x_wait(FIRST[ch] + k, dc)
        if ch == 0:
            for place in (1, 2):
                for dc in range(2):
                    x_copy(place, dc).start()
        rows = len(CHUNKS[ch]) * 2 * BLOCK
        start = FIRST[ch] * 2 * BLOCK
        for b in range(padded // 16):
            depth = min(LANES, rows - b * LANES)
            picked = jnp.dot(
                perm[:, :depth], raw[start + b * LANES : start + b * LANES + depth, :],
                preferred_element_type=F32,
            ).astype(BF16)
            for g in range(SECTORS):
                sends[ch][g * padded + 16 * b : g * padded + 16 * b + 16, :] = picked[16 * g : 16 * g + 16, :]
        for dz, rp in PLACES:
            zy_copy(ch, dz, rp).start()
        if ch == 0:
            spread_one(0, 0, 0)

    def spread(ch, dz):
        for rp in range(2):
            wait_for(landed(ch, dz, rp, True, half), zr.at[ch * 8 + dz * 2 + rp])
            pass_on(ch, dz, rp, "y").start()
            pass_on(ch, dz, rp, "c").start()

    def forward(ch, dz):
        for rp in range(2):
            wait_for(landed(ch, dz, rp, False, half), yr.at[ch * 8 + dz * 2 + rp])
            pass_on(ch, dz, rp, "f").start()

    def collect(ch, dz):
        height = 4 * PADDED[ch]
        rows = pl.ds(pl.multiple_of((z + 4 - dz) % 4 * height, 16), height)
        wait_for(gots[ch].at[rows, half_other], core_r.at[ch * 4 + dz])

    def multiply(ch, dz):
        height = 4 * PADDED[ch]
        rows = pl.ds(pl.multiple_of((z + 4 - dz) % 4 * height, 16), height)
        wide[:height, :] = jnp.dot(gots[ch][rows, :], v_ref[...], preferred_element_type=F32)

    def compact(ch, k):
        for side in range(2):

            @pl.when(yp == side)
            def _():
                for j in range(4):
                    to = Y_OF[side][j] * PAIR
                    start = j * PADDED[ch] + k * PAIR
                    prod[to : to + PAIR, :] = wide[start : start + PAIR, :]

    def encode(places, scale):
        tiles = WIDE // LANES // len(places)

        def biggest(i, m):
            rows = pl.ds(pl.multiple_of(i * 16, 16), 16)
            for j in range(WIDE // LANES):
                m = jnp.maximum(m, jnp.abs(prod[rows, j * LANES : (j + 1) * LANES]))
            return m

        top = lax.fori_loop(0, ZBLOCK // 16, biggest, jnp.full((16, LANES), 1e-30, F32))
        top = jnp.max(top, axis=0, keepdims=True)
        scale[...] = top * (1.0 / TOP)
        inv = TOP / top
        inv = jnp.broadcast_to(inv, (16, LANES))

        def code(i, _):
            rows = pl.ds(pl.multiple_of(i * 16, 16), 16)
            for j in range(WIDE // LANES):
                value = jnp.round(prod[rows, j * LANES : (j + 1) * LANES] * inv)
                at_tile = (j % tiles) * LANES
                places[j // tiles][rows, at_tile : at_tile + LANES] = value.astype(I32).astype(I16)
            return 0

        lax.fori_loop(0, ZBLOCK // 16, code, 0)

    def add(codes, scale, first, tiles):
        step = jnp.broadcast_to(scale[...], (16, LANES))

        def body(i, _):
            rows = pl.ds(pl.multiple_of(i * 16, 16), 16)
            for j in range(tiles):
                value = codes[rows, j * LANES : (j + 1) * LANES].astype(I32).astype(F32) * step
                prod[rows, (first + j) * LANES : (first + j + 1) * LANES] += value
            return 0

        lax.fori_loop(0, ZBLOCK // 16, body, 0)

    def far_copies(k, i):
        to = (x + 1 + 2 * k) % 4
        j = i * 2 + k
        make = functools.partial(pltpu.make_async_remote_copy, device_id=at(to, z, y, c), device_id_type=MESH)
        return (
            make(src_ref=far_out.at[j], dst_ref=far_in.at[j], send_sem=fas.at[0], recv_sem=far_.at[j]),
            make(src_ref=far_out_s.at[i], dst_ref=far_in_s.at[j], send_sem=fass.at[0], recv_sem=fars.at[j]),
        )

    def near_copies(k, i):
        to = (x + 1 + 2 * k) % 4
        j = i * 2 + k
        make = functools.partial(pltpu.make_async_remote_copy, device_id=at(to, z, y, c), device_id_type=MESH)
        return (
            make(src_ref=near_out.at[j], dst_ref=near_in.at[j], send_sem=nes.at[0], recv_sem=ner.at[j]),
            make(src_ref=near_out_s.at[j], dst_ref=near_in_s.at[j], send_sem=ness.at[0], recv_sem=ners.at[j]),
        )

    def plane(i):
        return i + i // 2 - 2 * (i // 3)

    def far_step(i, _):
        dz = plane(i)

        @pl.when(i < 3)
        def _():
            spread(0, plane(i + 1))

        forward(0, dz)
        collect(0, dz)
        multiply(0, dz)
        compact(0, 0)
        encode((far_out.at[i * 2], far_out.at[i * 2 + 1]), far_out_s.at[i])
        for k in range(2):
            for copy in far_copies(k, i):
                copy.start()

        @pl.when(i == 1)
        def _():
            choose(1)

        @pl.when(i >= 2)
        def _():
            spread(1, plane(i - 2))

        return 0

    def near_step(i, _):
        dz = plane(i)

        @pl.when(i < 2)
        def _():
            spread(1, plane(i + 2))

        forward(1, dz)
        collect(1, dz)
        multiply(1, dz)
        for k in range(2):
            j = i * 2 + k
            compact(1, k)
            wait_for(far_in.at[j], far_.at[j])
            wait_for(far_in_s.at[j], fars.at[j])
            add(far_in.at[j], far_in_s.at[j], k * 7, 7)
            encode((near_out.at[j],), near_out_s.at[j])
            for copy in near_copies(k, i):
                copy.start()

        @pl.when(i == 0)
        def _():
            choose(2)

        @pl.when(i >= 1)
        def _():
            spread(2, plane(i - 1))

        return 0

    def out_copy(i):
        rows = pl.ds(pl.multiple_of((z + 4 - plane(i)) % 4 * ZBLOCK, 16), ZBLOCK)
        return pltpu.make_async_copy(done.at[i], out_ref.at[rows, :], out_sem.at[0])

    def finish(i):
        left, right = i * 2, i * 2 + 1
        steps = [jnp.broadcast_to(near_in_s[j], (16, LANES)) for j in (left, right)]

        def body(n, _):
            rows = pl.ds(pl.multiple_of(n * 16, 16), 16)
            for j in range(WIDE // LANES):
                cols = slice(j * LANES, (j + 1) * LANES)
                total = prod[rows, cols]
                for m, step in zip((left, right), steps):
                    total += near_in[m, rows, cols].astype(I32).astype(F32) * step
                done[i, rows, cols] = total.astype(BF16)
            return 0

        lax.fori_loop(0, ZBLOCK // 16, body, 0)

    def last_step(i, _):
        dz = plane(i)

        @pl.when(i == 0)
        def _():
            spread(2, plane(3))

        forward(2, dz)
        collect(2, dz)
        multiply(2, dz)
        compact(2, 0)
        for k in range(2):
            j = i * 2 + k
            wait_for(near_in.at[j], ner.at[j])
            wait_for(near_in_s.at[j], ners.at[j])
        finish(i)
        out_copy(i).start()
        return 0

    choose(0)
    spread_one(0, 0, 1)
    for dc in range(2):
        x_copy(3, dc).start()
    lax.fori_loop(0, 4, far_step, 0)
    lax.fori_loop(0, 4, near_step, 0)
    lax.fori_loop(0, 4, last_step, 0)

    wait_for(raw.at[: 7 * BLOCK, :], xs.at[0])
    for ch in range(3):
        wait_for(sends[ch].at[: 7 * PADDED[ch], :], zs.at[ch])
        for sem in (cs, ys, fs):
            wait_for(sends[ch], sem.at[ch])
    wait_for(far_out, fas.at[0])
    wait_for(near_out, nes.at[0])
    wait_for(near_out_s, fass.at[0])
    wait_for(near_out_s, ness.at[0])
    wait_for(done, out_sem.at[0])


Y_OF = ((0, 3, 1, 2), (2, 1, 3, 0))
PLACES = ((0, 0), (0, 1), (1, 0), (3, 0), (1, 1), (3, 1), (2, 0), (2, 1))


def per_device(amplitudes, integrals, nonzero_tile_count, sector_owner):
    dma = pltpu.SemaphoreType.DMA
    vmem = pltpu.VMEM
    codes = [vmem((8, ZBLOCK, cols), I16) for cols in (HALF, HALF, WIDE, WIDE)]
    scales = [vmem((n, 1, LANES), F32) for n in (4, 8, 8, 8)]
    out = pl.pallas_call(
        kernel,
        out_shape=jax.ShapeDtypeStruct((4 * ZBLOCK, WIDE), BF16),
        in_specs=[
            pl.BlockSpec(memory_space=pltpu.HBM),
            pl.BlockSpec(memory_space=pltpu.HBM),
            pl.BlockSpec(memory_space=pltpu.HBM),
            pl.BlockSpec(memory_space=pltpu.HBM),
        ],
        out_specs=pl.BlockSpec(memory_space=pl.ANY),
        scratch_shapes=[
            pltpu.SMEM((SECTORS,), I32),
            pltpu.SMEM((SECTORS,), I32),
            dma((2,)),
            vmem((8 * BLOCK, HALF), BF16),
            *[vmem((SECTORS * p, HALF), BF16) for p in PADDED],
            *[vmem((16 * p, WIDE), BF16) for p in PADDED],
            vmem((WIDE, WIDE), BF16),
            vmem((LANES, LANES), BF16),
            vmem((4 * max(PADDED), WIDE), F32),
            vmem((ZBLOCK, WIDE), F32),
            vmem((4, ZBLOCK, WIDE), BF16),
            dma((1,)),
            *codes,
            *scales,
            *[dma((n,)) for n in (1, 1, 8, 3, 3, 3, 3, 24, 24, 12)],
            *[dma((n,)) for n in (1, 8) * 4],
        ],
        compiler_params=pltpu.CompilerParams(
            collective_id=0, has_side_effects=True, vmem_limit_bytes=51 * 1024 * 1024
        ),
        cost_estimate=pl.CostEstimate(
            flops=2 * 16 * ZBLOCK * WIDE * WIDE, bytes_accessed=20_000_000, transcendentals=0
        ),
    )(
        pltpu.with_memory_space_constraint(nonzero_tile_count, pltpu.HBM),
        pltpu.with_memory_space_constraint(sector_owner, pltpu.HBM),
        amplitudes.reshape(BLOCK, amplitudes.shape[2]),
        integrals.reshape(WIDE, WIDE),
    )
    return out[:, None, :]


def solution(mesh):
    in_specs = (P(("vir", "occ"), None, None), P("occ", "vir", None), P(), P())
    out_specs = P("vir", "occ", None)
    return jax.shard_map(
        per_device, mesh=mesh, in_specs=in_specs, out_specs=out_specs, check_vma=False
    )
```
